32 devices in a mesh: leaf: 16 (over z, y, x), sec: 2 (over core).
Axes of the slice: x: 2, y: 2, z: 4, core: 2. Of those that a mesh axis runs over, the one named last changes fastest.
Arguments:
- leaf_inv: bfloat16 [32768, 1024], P(('leaf', 'sec')), may hold values from -0.1875 to 0.1875
- subtree_blocks: int32 [16, 2], P('leaf', 'sec'), may hold values from 1 to 8
- subtree_shift_rhs: bfloat16 [32768, 128], P(('leaf', 'sec')), may hold values from -6 to 6
- leaf_noise: bfloat16 [32768, 128], P(('leaf', 'sec')), may hold values from -6 to 6
- leaf_dev: bfloat16 [32768], P(('leaf', 'sec')), may hold values from 0.29882812 to 3
- sep_inv: bfloat16 [1024, 896], P(('leaf', 'sec')), may hold values from -0.375 to 0.375
- sep_panel: bfloat16 [1024, 896], P(('leaf', 'sec')), may hold values from -0.375 to 0.375
- sep_rhs: bfloat16 [3, 1024, 128], P(None, ('leaf', 'sec')), may hold values from -6 to 6
- sep_noise: bfloat16 [3, 1024, 128], P(None, ('leaf', 'sec')), may hold values from -6 to 6
- sep_dev: bfloat16 [3, 1024], P(None, ('leaf', 'sec')), may hold values from 0.29882812 to 3
Outputs:
- subtree_scaled_samples: bfloat16 [32768, 128], P(('leaf', 'sec'))
- sep_sample: bfloat16 [3, 1024, 128], P(None, ('leaf', 'sec'))
The draws below stay inside these ranges and needn't reach their ends.
All inputs are finite; a program needn't handle non-finite values.
Results may differ from the reference program's by a relative error of at most 0.019.
Values may be sent and summed in bfloat16 or wider, within the bound.
No kernel may reach another device: no remote copies, remote signals or barrier semaphores. Data moves between devices by JAX's collectives and lax.ppermute only.
A program may use at most 64 MiB of HBM per device.

```python
import math
import jax
import jax.numpy as jnp
from jax import lax

SUBTREE_ROWS = 1024
SEP_DEV = 32
SAMPLE_COUNT = 128
LEVELS = 3
BLOCK = 128
LEAF_ROWS = 32768
SEP_ROWS = 1024
PANEL_COLS = 896
N_LEAF = 16
N_SEC = 2


def place_ends(drawn, stream_key, low, high):
    place = [jax.random.randint(jax.random.fold_in(stream_key, axis), (), 0, length) for axis, length in enumerate(drawn.shape)]
    main_axis = drawn.shape.index(max(drawn.shape))
    beside = place[:main_axis] + [(place[main_axis] + 1) % drawn.shape[main_axis]] + place[main_axis + 1:]
    return drawn.at[tuple(place)].set(low).at[tuple(beside)].set(high)


def steps_of(rng, dims, cuts, low, high):
    factor_of = 1.0
    for position, blocks in cuts:
        draws = jax.random.uniform(jax.random.fold_in(jax.random.fold_in(rng, 6), position), (blocks,), jnp.float32, low / len(cuts), high / len(cuts))
        factor_of = factor_of * jnp.repeat(jnp.exp(draws), dims[position] // blocks).reshape((-1,) + (1,) * (len(dims) - 1 - position))
    return factor_of


def normal_values(rng, dims, deviation, bound, cuts=(), kind=jnp.bfloat16):
    values = jax.random.normal(rng, dims, jnp.float32) * deviation
    if len(cuts) > 0:
        values = steps_of(rng, dims, cuts, -0.22, 0.18) * values
    return jnp.clip(values, min=-bound, max=bound).astype(kind)


def setup_inputs(seed: int = 0) -> dict:
    key_of = jax.random.split(jax.random.key(seed), 11)
    return {
        "leaf_inv": normal_values(key_of[0], (LEAF_ROWS, SUBTREE_ROWS), SUBTREE_ROWS ** -0.5, 0.1875, ((0, 32),)),
        "subtree_blocks": place_ends(jax.random.randint(key_of[1], (N_LEAF, N_SEC), 1, SUBTREE_ROWS // BLOCK + 1), jax.random.fold_in(key_of[1], 1), 1, (SUBTREE_ROWS // BLOCK + 1) - 1).astype(jnp.int32),
        "subtree_shift_rhs": normal_values(key_of[2], (LEAF_ROWS, SAMPLE_COUNT), 1.0, 6.0, ((0, 32),)),
        "leaf_noise": normal_values(key_of[3], (LEAF_ROWS, SAMPLE_COUNT), 1.0, 6.0, ((0, 32),)),
        "leaf_dev": jnp.clip(jnp.exp(math.log(3.0) - 2.306499 * jax.random.uniform(key_of[4], (LEAF_ROWS,), jnp.float32) ** steps_of(key_of[4], (LEAF_ROWS,), ((0, 32),), -0.2, 0.2)), 0.29882812, 3.0).astype(jnp.bfloat16),
        "sep_inv": normal_values(key_of[5], (SEP_ROWS, PANEL_COLS), (4 * N_SEC * SEP_DEV) ** -0.5, 0.375, ((0, 32),)),
        "sep_panel": normal_values(key_of[6], (SEP_ROWS, PANEL_COLS), (4 * N_SEC * SEP_DEV) ** -0.5, 0.375, ((0, 32),)),
        "sep_rhs": normal_values(key_of[7], (LEVELS, SEP_ROWS, SAMPLE_COUNT), 1.0, 6.0, ((1, 32),)),
        "sep_noise": normal_values(key_of[8], (LEVELS, SEP_ROWS, SAMPLE_COUNT), 1.0, 6.0, ((1, 32),)),
        "sep_dev": jnp.clip(jnp.exp(math.log(3.0) - 2.306499 * jax.random.uniform(key_of[9], (LEVELS, SEP_ROWS), jnp.float32) ** steps_of(key_of[9], (LEVELS, SEP_ROWS), ((1, 32),), -0.2, 0.2)), 0.29882812, 3.0).astype(jnp.bfloat16),
    }


def subtree_forward(matrix_entries):
    inverse_block, mean_shifted, row_activity = matrix_entries
    block_product = jnp.dot(inverse_block, mean_shifted, preferred_element_type=jnp.float32)
    return jnp.where(row_activity, block_product, jnp.float32(0.0)).astype(jnp.bfloat16)


def sep_forward(matrix_entries):
    panel, inverse_block, mean_shifted, children = matrix_entries
    reduced = (mean_shifted.astype(jnp.float32) - jnp.dot(panel, children, preferred_element_type=jnp.float32)).astype(jnp.bfloat16)
    return jnp.dot(inverse_block, reduced, preferred_element_type=jnp.float32).astype(jnp.bfloat16)


def solve_back(matrix_entries):
    inverse_block, vector = matrix_entries
    return jnp.dot(inverse_block.T, vector, preferred_element_type=jnp.float32).astype(jnp.bfloat16)


def push_down(matrix_entries):
    panel, vector = matrix_entries
    return jnp.dot(panel.T, vector, preferred_element_type=jnp.float32)


def leaf_back(matrix_entries):
    inverse_block, vector = matrix_entries
    return jnp.dot(inverse_block.T, vector, preferred_element_type=jnp.float32)


def reference(leaf_inv, subtree_blocks, subtree_shift_rhs, leaf_noise, leaf_dev, sep_inv, sep_panel, sep_rhs, sep_noise, sep_dev):
    device_list = N_LEAF * N_SEC
    active_rows = subtree_blocks.reshape(device_list).astype(jnp.int32) * BLOCK
    row_positions = jnp.arange(SUBTREE_ROWS, dtype=jnp.int32)
    row_activity = (row_positions[None, :] >= (SUBTREE_ROWS - active_rows)[:, None])[:, :, None]
    inverse_subtree = leaf_inv.reshape(device_list, SUBTREE_ROWS, SUBTREE_ROWS)
    subtree_rhs_block = jnp.where(row_activity, subtree_shift_rhs.reshape(device_list, SUBTREE_ROWS, SAMPLE_COUNT), jnp.zeros((), subtree_shift_rhs.dtype))
    subtree_forward_solution = lax.map(subtree_forward, (inverse_subtree, subtree_rhs_block, row_activity))
    top = subtree_forward_solution[:, SUBTREE_ROWS - SEP_DEV:, :].reshape(device_list * SEP_DEV, SAMPLE_COUNT)
    solved = []
    for height in range(1, LEVELS + 1):
        span = 2 ** height * N_SEC * SEP_DEV
        offset = (2 ** height - 2) * N_SEC * SEP_DEV
        groups = device_list * SEP_DEV // span
        panel = sep_panel[:, offset:offset + span].reshape(groups, span, span)
        inverse_block = sep_inv[:, offset:offset + span].reshape(groups, span, span)
        mean_shifted = sep_rhs[height - 1].reshape(groups, span, SAMPLE_COUNT)
        children = top.reshape(groups, span, SAMPLE_COUNT)
        result = lax.map(sep_forward, (panel, inverse_block, mean_shifted, children)).reshape(device_list * SEP_DEV, SAMPLE_COUNT)
        solved.append(result)
        top = result
    samples = [None] * LEVELS
    correction = jnp.zeros((device_list * SEP_DEV, SAMPLE_COUNT), jnp.float32)
    for height in range(LEVELS, 0, -1):
        span = 2 ** height * N_SEC * SEP_DEV
        offset = (2 ** height - 2) * N_SEC * SEP_DEV
        groups = device_list * SEP_DEV // span
        panel = sep_panel[:, offset:offset + span].reshape(groups, span, span)
        inverse_block = sep_inv[:, offset:offset + span].reshape(groups, span, span)
        summed = solved[height - 1].astype(jnp.float32) + sep_noise[height - 1].astype(jnp.float32) - correction
        vector = summed.astype(jnp.bfloat16).reshape(groups, span, SAMPLE_COUNT)
        backed = lax.map(solve_back, (inverse_block, vector))
        flat = backed.reshape(device_list * SEP_DEV, SAMPLE_COUNT)
        samples[height - 1] = (sep_dev[height - 1][:, None].astype(jnp.float32) * flat.astype(jnp.float32)).astype(jnp.bfloat16)
        correction = lax.map(push_down, (panel, backed)).reshape(device_list * SEP_DEV, SAMPLE_COUNT)
    boundary = correction.reshape(device_list, SEP_DEV, SAMPLE_COUNT)
    leading = jnp.zeros((device_list, SUBTREE_ROWS - SEP_DEV, SAMPLE_COUNT), jnp.float32)
    placed = jnp.concatenate([leading, boundary], axis=1)
    noise_leaf = leaf_noise.reshape(device_list, SUBTREE_ROWS, SAMPLE_COUNT)
    subtree_summed = subtree_forward_solution.astype(jnp.float32) + noise_leaf.astype(jnp.float32) - placed
    subtree_weight = jnp.where(row_activity, subtree_summed, jnp.float32(0.0)).astype(jnp.bfloat16)
    subtree_solution = lax.map(leaf_back, (inverse_subtree, subtree_weight))
    sample_scales = leaf_dev.reshape(device_list, SUBTREE_ROWS, 1).astype(jnp.float32)
    subtree_scaled_samples = jnp.where(row_activity, sample_scales * subtree_solution, jnp.float32(0.0)).astype(jnp.bfloat16).reshape(device_list * SUBTREE_ROWS, SAMPLE_COUNT)
    return subtree_scaled_samples, jnp.stack(samples)
```

```python
import functools

import jax
import jax.numpy as jnp
from jax import lax
from jax.experimental import pallas as pl
from jax.experimental.pallas import tpu as pltpu
from jax.sharding import PartitionSpec as P

BLOCK = 128
VMEM_LIMIT = 56 * 2**20
AXES = ("leaf", "sec")


def to_chips(block, distances):
    leaves, sections = lax.axis_size("leaf"), lax.axis_size("sec")
    route = []
    for leaf in range(leaves):
        for section, distance in enumerate(distances):
            route.append((leaf * sections + section, (leaf ^ distance) * sections + section))
    return lax.ppermute(block, AXES, route)


def to_sections(block, turn):
    sections = lax.axis_size("sec")
    return lax.ppermute(block, "sec", [(s, (s - turn) % sections) for s in range(sections)])


def pack_kernel(levels, blocks_ref, leaf_ref, shift_ref, panel_ref, inv_ref, rhs_ref, noise_ref, low_ref, top_ref):
    row_count, samples = low_ref.shape[0], shift_ref.shape[1]
    subtree_rows = shift_ref.shape[0]
    live_from = subtree_rows - blocks_ref[0, 0] * BLOCK
    positions = lax.broadcasted_iota(jnp.int32, shift_ref.shape, 0)
    shift = shift_ref[...]
    shift = jnp.where(positions >= live_from, shift, jnp.zeros_like(shift))
    boundary = jnp.dot(leaf_ref[...], shift, preferred_element_type=jnp.float32)
    low_ref[:, :samples] = boundary.astype(jnp.bfloat16)
    at = samples
    offset = 0
    unit = panel_ref.shape[1] // (2 ** (levels + 1) - 2)
    for height in range(1, levels + 1):
        span = 2**height * unit
        out = low_ref if height < levels else top_ref
        if height == levels:
            at = 0
        out[:, at : at + span] = panel_ref[:, offset : offset + span]
        out[:, at + span : at + 2 * span] = inv_ref[:, offset : offset + span]
        out[:, at + 2 * span : at + 2 * span + samples] = rhs_ref[height - 1]
        out[:, at + 2 * span + samples : at + 2 * span + 2 * samples] = noise_ref[height - 1]
        at += 2 * span + 2 * samples
        offset += span


def place(pieces_meta, piece_refs, place_ref, whole_ref, row_count):
    for index, (which, start) in enumerate(pieces_meta):
        at = pl.multiple_of(place_ref[index], row_count)
        whole_ref[pl.ds(at, row_count), :] = piece_refs[which][start : start + row_count, :]


def solve_forward(whole, rows, at, span, samples, children):
    panel = whole[rows, at : at + span]
    inverse = whole[rows, at + span : at + 2 * span]
    rhs = whole[rows, at + 2 * span : at + 2 * span + samples]
    reduced = rhs.astype(jnp.float32) - jnp.dot(panel, children, preferred_element_type=jnp.float32)
    reduced = reduced.astype(jnp.bfloat16)
    return jnp.dot(inverse, reduced, preferred_element_type=jnp.float32).astype(jnp.bfloat16)


def low_kernel(levels, unit, pieces_meta, place_ref, *refs):
    piece_refs, (whole_ref, *solved_refs) = refs[: -levels], refs[-levels:]
    row_count = whole_ref.shape[0] // sum(1 for _ in pieces_meta)
    place(pieces_meta, piece_refs, place_ref, whole_ref, row_count)
    samples = solved_refs[0].shape[1]
    total = whole_ref.shape[0]
    below_ref, below_at = whole_ref, 0
    at = samples
    for height in range(1, levels):
        span = 2**height * unit
        for group in range(total // span):
            rows = slice(group * span, (group + 1) * span)
            children = below_ref[rows, 0:samples]
            solved_refs[height - 1][rows, :] = solve_forward(whole_ref, rows, at, span, samples, children)
        below_ref = solved_refs[height - 1]
        at += 2 * span + 2 * samples


def transposed_dot(matrix, vector):
    return lax.dot_general(matrix, vector, (((0,), (0,)), ((), ())), preferred_element_type=jnp.float32)


def top_kernel(levels, unit, pieces_meta, place_ref, low_ref, dev_ref, partner_ref, *refs):
    solved_refs = refs[: levels - 1]
    sample_ref, correction_ref, whole_ref, child_ref, sum_ref, x_ref = refs[-6:]
    piece_refs = refs[levels - 1 : -6]
    samples = partner_ref.shape[1]
    count = len(pieces_meta)
    row_count = whole_ref.shape[0] // count
    place(pieces_meta, piece_refs, place_ref, whole_ref, row_count)
    half = child_ref.shape[0] // 2
    upper = place_ref[count]
    child_ref[pl.ds(pl.multiple_of(upper * half, half), half), :] = solved_refs[-1][...]
    child_ref[pl.ds(pl.multiple_of((1 - upper) * half, half), half), :] = partner_ref[...]
    span = 2**levels * unit
    rows = slice(0, span)
    own = solve_forward(whole_ref, rows, 0, span, samples, child_ref[...])
    correction = None
    low_at = low_ref.shape[1]
    for height in range(levels, 0, -1):
        span = 2**height * unit
        first = pl.multiple_of(place_ref[count + 1 + 2 * (height - 1)], span)
        mine = pl.multiple_of(place_ref[count + 2 + 2 * (height - 1)], row_count)
        if height == levels:
            source, at, rows = whole_ref, 0, pl.ds(0, span)
        else:
            low_at -= 2 * span + 2 * samples
            source, at, rows = low_ref, low_at, pl.ds(first, span)
            own = solved_refs[height - 1][rows, :]
        summed = own.astype(jnp.float32) + source[rows, at + 2 * span + samples : at + 2 * span + 2 * samples].astype(
            jnp.float32
        )
        if correction is not None:
            summed = summed - correction
        x = transposed_dot(source[rows, at + span : at + 2 * span], summed.astype(jnp.bfloat16))
        x = x.astype(jnp.bfloat16)
        x_ref[0:span, :] = x
        sample_ref[height - 1] = (
            dev_ref[height - 1].astype(jnp.float32) * x_ref[pl.ds(mine, row_count), :].astype(jnp.float32)
        ).astype(jnp.bfloat16)
        sum_ref[0:span, :] = transposed_dot(source[rows, at : at + span], x)
        if height > 1:
            below = pl.multiple_of(place_ref[count + 1 + 2 * levels + height - 1], span // 2)
            correction = sum_ref[pl.ds(below, span // 2), :]
        else:
            correction_ref[...] = sum_ref[pl.ds(mine, row_count), :]


def from_partner(block, axis, apart):
    count = lax.axis_size(axis)
    route = []
    for low in range(count):
        high = low | 1 << apart
        if high != low and high < count:
            route += [(low, high), (high, low)]
    return lax.ppermute(block, axis, route)


def pair_gather(block, height):
    leaf_place = lax.axis_index("leaf")
    for bit_index in range(height):
        partner = from_partner(block, "leaf", bit_index)
        upper_half = leaf_place >> bit_index & 1 == 1
        block = jnp.where(
            upper_half, jnp.concatenate([partner, block], 0), jnp.concatenate([block, partner], 0)
        )
    return block


def group_gather(piece, height):
    block = lax.all_gather(piece, "sec", axis=0, tiled=True)
    return pair_gather(block, height)


def halve_pairs(partial_sum, height):
    leaf_place = lax.axis_index("leaf")
    for bit_index in reversed(range(height)):
        half_rows = partial_sum.shape[0] // 2
        lower_rows = partial_sum[:half_rows]
        upper_rows = partial_sum[half_rows:]
        upper_half = leaf_place >> bit_index & 1 == 1
        kept = jnp.where(upper_half, upper_rows, lower_rows)
        outgoing = jnp.where(upper_half, lower_rows, upper_rows)
        partial_sum = kept + from_partner(outgoing, "leaf", bit_index)
    return partial_sum


def group_reduce(partial_sum, height):
    reduced = halve_pairs(partial_sum, height)
    return lax.psum_scatter(reduced, "sec", scatter_dimension=0, tiled=True)


def leafwise_on_device(
    leaf_inv,
    subtree_blocks,
    subtree_shift_rhs,
    leaf_noise,
    leaf_dev,
    sep_inv,
    sep_panel,
    sep_rhs,
    sep_noise,
    sep_dev,
):
    subtree_row_count = leaf_inv.shape[0]
    row_count = sep_inv.shape[0]
    levels = sep_rhs.shape[0]
    sections = lax.axis_size("sec")
    active_rows = subtree_blocks[0, 0] * BLOCK
    row_positions = jnp.arange(subtree_row_count, dtype=jnp.int32)
    row_activity = (row_positions >= subtree_row_count - active_rows)[:, None]
    subtree_shifted = jnp.where(
        row_activity, subtree_shift_rhs, jnp.zeros((), subtree_shift_rhs.dtype)
    )
    forward_subtree = jnp.dot(leaf_inv, subtree_shifted, preferred_element_type=jnp.float32)
    subtree_forward_solution = jnp.where(row_activity, forward_subtree, jnp.float32(0.0)).astype(
        jnp.bfloat16
    )
    top = subtree_forward_solution[subtree_row_count - row_count :]
    solved = []
    for height in range(1, levels + 1):
        span = 2**height * sections * row_count
        offset = (2**height - 2) * sections * row_count
        children = group_gather(top, height)
        panel = sep_panel[:, offset : offset + span]
        inverse_block = sep_inv[:, offset : offset + span]
        reduced = (
            sep_rhs[height - 1].astype(jnp.float32)
            - jnp.dot(panel, children, preferred_element_type=jnp.float32)
        ).astype(jnp.bfloat16)
        whole_reduced = group_gather(reduced, height)
        result = jnp.dot(inverse_block, whole_reduced, preferred_element_type=jnp.float32).astype(
            jnp.bfloat16
        )
        solved.append(result)
        top = result
    samples = [None] * levels
    correction = None
    for height in range(levels, 0, -1):
        span = 2**height * sections * row_count
        offset = (2**height - 2) * sections * row_count
        panel = sep_panel[:, offset : offset + span]
        inverse_block = sep_inv[:, offset : offset + span]
        summed = solved[height - 1].astype(jnp.float32) + sep_noise[height - 1].astype(jnp.float32)
        if correction is not None:
            summed = summed - correction
        vector = summed.astype(jnp.bfloat16)
        backed = group_reduce(transposed_dot(inverse_block, vector), height).astype(
            jnp.bfloat16
        )
        samples[height - 1] = (
            sep_dev[height - 1][:, None].astype(jnp.float32) * backed.astype(jnp.float32)
        ).astype(jnp.bfloat16)
        correction = group_reduce(transposed_dot(panel, backed), height)
    leading = jnp.zeros((subtree_row_count - row_count, correction.shape[1]), jnp.float32)
    placed = jnp.concatenate([leading, correction], axis=0)
    subtree_summed = (
        subtree_forward_solution.astype(jnp.float32) + leaf_noise.astype(jnp.float32) - placed
    )
    subtree_weight = jnp.where(row_activity, subtree_summed, jnp.float32(0.0)).astype(jnp.bfloat16)
    subtree_solution = transposed_dot(leaf_inv, subtree_weight)
    sample_scales = leaf_dev[:, None].astype(jnp.float32)
    subtree_scaled_samples = jnp.where(
        row_activity, sample_scales * subtree_solution, jnp.float32(0.0)
    ).astype(jnp.bfloat16)
    return (subtree_scaled_samples, jnp.stack(samples))


def split_pieces(pieces):
    arrays, meta, where = [], [], []
    for array, start, distance, section in pieces:
        for index, known in enumerate(arrays):
            if known is array:
                break
        else:
            arrays.append(array)
            index = len(arrays) - 1
        meta.append((index, start))
        where.append((distance, section))
    return arrays, meta, where


def row_places(where, leaves, leaf, sections, row_count):
    return [(((leaf ^ distance) & (leaves - 1)) * sections + section) * row_count for distance, section in where]


def on_device(
    leaf_inv,
    subtree_blocks,
    subtree_shift_rhs,
    leaf_noise,
    leaf_dev,
    sep_inv,
    sep_panel,
    sep_rhs,
    sep_noise,
    sep_dev,
):
    subtree_rows = leaf_inv.shape[0]
    row_count = sep_inv.shape[0]
    levels, _, samples = sep_rhs.shape
    sections = lax.axis_size("sec")
    unit = sections * row_count
    leaf = lax.axis_index("leaf")
    section = lax.axis_index("sec")
    params = pltpu.CompilerParams(vmem_limit_bytes=VMEM_LIMIT)
    vmem = pl.BlockSpec(memory_space=pltpu.VMEM)
    smem = pl.BlockSpec(memory_space=pltpu.SMEM)

    top_columns = 2 * 2**levels * unit + 2 * samples
    low_columns = samples + sum(2 * 2**h * unit + 2 * samples for h in range(1, levels))
    full = lambda array: pl.BlockSpec(array.shape, lambda i: (0,) * array.ndim)
    low, top = pl.pallas_call(
        functools.partial(pack_kernel, levels),
        grid=(1,),
        out_shape=(
            jax.ShapeDtypeStruct((row_count, low_columns), jnp.bfloat16),
            jax.ShapeDtypeStruct((row_count, top_columns), jnp.bfloat16),
        ),
        in_specs=[
            smem,
            pl.BlockSpec((row_count, subtree_rows), lambda i: (subtree_rows // row_count - 1, 0)),
            full(subtree_shift_rhs),
            full(sep_panel),
            full(sep_inv),
            full(sep_rhs),
            full(sep_noise),
        ],
        out_specs=(
            pl.BlockSpec((row_count, low_columns), lambda i: (0, 0)),
            pl.BlockSpec((row_count, top_columns), lambda i: (0, 0)),
        ),
        compiler_params=params,
        name="pack",
    )(subtree_blocks, leaf_inv, subtree_shift_rhs, sep_panel, sep_inv, sep_rhs, sep_noise)

    quad = 2 ** (levels - 1)
    group = 2**levels
    other = 1 - section

    def swap(block):
        return to_sections(block, 1)

    low_other, top_other = swap(low), swap(top)
    low_pair = jnp.concatenate([low, low_other], axis=0)
    top_pair = jnp.concatenate([top, top_other], axis=0)

    def halves(block, distance):
        arrived = to_chips(block, (distance, distance))
        return [(arrived, 0, distance, section), (swap(arrived), 0, distance, other)]

    def pairs(block, first, second):
        arrived = to_chips(block, (first, second))
        passed = swap(arrived)
        here = jnp.where(section == 0, first, second)
        there = jnp.where(section == 0, second, first)
        return [
            (arrived, 0, here, section),
            (arrived, row_count, here, other),
            (passed, 0, there, other),
            (passed, row_count, there, section),
        ]

    top_pieces = [(top, 0, 0, section), (top_other, 0, 0, other)]
    low_pieces = [(low, 0, 0, section), (low_other, 0, 0, other)]
    top_pieces += halves(top, 4)
    low_pieces += pairs(low_pair, 1, 2)
    low_pieces += halves(low, 3)
    top_pieces += pairs(top_pair, 5, 6)
    top_pieces += pairs(top_pair, 7, 1)
    top_pieces += pairs(top_pair, 2, 3)

    arrays, meta, where = split_pieces(low_pieces)
    places = jnp.stack(row_places(where, quad, leaf, sections, row_count)).astype(jnp.int32)
    low_whole, *solved = pl.pallas_call(
        functools.partial(low_kernel, levels, unit, meta),
        out_shape=[jax.ShapeDtypeStruct((quad * unit, low_columns), jnp.bfloat16)]
        + [jax.ShapeDtypeStruct((quad * unit, samples), jnp.bfloat16)] * (levels - 1),
        in_specs=[smem] + [vmem] * len(arrays),
        out_specs=[vmem] * levels,
        compiler_params=params,
        name="low",
    )(places, *arrays)
    partner = to_chips(solved[-1], (quad,) * sections)

    row_positions = jnp.arange(subtree_rows, dtype=jnp.int32)
    row_activity = (row_positions >= subtree_rows - subtree_blocks[0, 0] * BLOCK)[:, None]
    zero = jnp.float32(0.0)
    shifted = jnp.where(row_activity, subtree_shift_rhs, jnp.zeros((), subtree_shift_rhs.dtype))
    forward = jnp.dot(leaf_inv, shifted, preferred_element_type=jnp.float32)
    forward = jnp.where(row_activity, forward, zero).astype(jnp.bfloat16)

    arrays, meta, where = split_pieces(top_pieces)
    places = row_places(where, group, leaf, sections, row_count)
    places.append(leaf >> (levels - 1) & 1)
    for height in range(1, levels + 1):
        places.append(((leaf & (quad - 1)) >> height << height) * unit if height < levels else 0 * leaf)
        places.append((leaf & (2**height - 1)) * unit + section * row_count)
    for height in range(1, levels + 1):
        places.append((leaf >> (height - 1) & 1) * 2 ** (height - 1) * unit)
    places = jnp.stack(places).astype(jnp.int32)
    span = group * unit
    sep_sample, correction = pl.pallas_call(
        functools.partial(top_kernel, levels, unit, meta),
        out_shape=(
            jax.ShapeDtypeStruct((levels, row_count, samples), jnp.bfloat16),
            jax.ShapeDtypeStruct((row_count, samples), jnp.float32),
        ),
        in_specs=[smem] + [vmem] * (2 + levels + len(arrays)),
        out_specs=(vmem, vmem),
        scratch_shapes=[
            pltpu.VMEM((span, top_columns), jnp.bfloat16),
            pltpu.VMEM((span, samples), jnp.bfloat16),
            pltpu.VMEM((span, samples), jnp.float32),
            pltpu.VMEM((span, samples), jnp.bfloat16),
        ],
        compiler_params=params,
        name="top",
    )(places, low_whole, jnp.broadcast_to(sep_dev[:, :, None], sep_rhs.shape), partner, *solved, *arrays)

    leading = jnp.zeros((subtree_rows - row_count, samples), jnp.float32)
    placed = jnp.concatenate([leading, correction], axis=0)
    summed = forward.astype(jnp.float32) + leaf_noise.astype(jnp.float32) - placed
    weight = jnp.where(row_activity, summed, zero).astype(jnp.bfloat16)
    solution_rows = transposed_dot(leaf_inv, weight)
    scaled = leaf_dev[:, None].astype(jnp.float32) * solution_rows
    return jnp.where(row_activity, scaled, zero).astype(jnp.bfloat16), sep_sample


def solution(mesh):
    rows = P(AXES, None)
    in_specs = (
        rows,
        P("leaf", "sec"),
        rows,
        rows,
        P(AXES),
        rows,
        rows,
        P(None, AXES, None),
        P(None, AXES, None),
        P(None, AXES),
    )
    out_specs = (rows, P(None, AXES, None))
    paired = mesh.shape["sec"] == 2 and mesh.shape["leaf"] % 8 == 0
    program = on_device if paired else leafwise_on_device
    return jax.shard_map(program, mesh=mesh, in_specs=in_specs, out_specs=out_specs, check_vma=False)
```

```python
import functools

import jax
import jax.numpy as jnp
from jax import lax
from jax.experimental import pallas as pl
from jax.experimental.pallas import tpu as pltpu
from jax.sharding import PartitionSpec as P

BLOCK = 128
AXES = ("leaf", "sec")


def to_chips(block, distances):
    leaves, sections = lax.axis_size("leaf"), lax.axis_size("sec")
    route = []
    for leaf in range(leaves):
        for section, distance in enumerate(distances):
            route.append((leaf * sections + section, (leaf ^ distance) * sections + section))
    return lax.ppermute(block, AXES, route)


def column_of(row):
    count = row.shape[1]
    across = lax.broadcasted_iota(jnp.int32, (count, count), 1)
    down = lax.broadcasted_iota(jnp.int32, (count, count), 0)
    return jnp.sum(jnp.where(across == down, row, jnp.zeros_like(row)), axis=1, keepdims=True)


def live_rows(blocks_ref, rows, columns):
    live_from = rows - blocks_ref[0:1, 0:columns] * BLOCK
    return lax.broadcasted_iota(jnp.int32, (rows, columns), 0) >= live_from


def pack_kernel(
    levels,
    blocks_ref,
    leaf_ref,
    shift_ref,
    panel_ref,
    inv_ref,
    rhs_ref,
    noise_ref,
    pack_ref,
    edge_ref,
    moved_ref,
    arrived,
):
    row_count, samples = edge_ref.shape[0], shift_ref.shape[1]
    subtree_rows = shift_ref.shape[0]
    copies = [
        pltpu.make_async_copy(shift_ref, moved_ref, arrived.at[0]),
        pltpu.make_async_copy(leaf_ref.at[pl.ds(subtree_rows - row_count, row_count)], edge_ref, arrived.at[1]),
    ]
    at, offset = samples, 0
    unit = panel_ref.shape[1] // (2 ** (levels + 1) - 2)
    for height in range(1, levels + 1):
        span = 2**height * unit
        for source, width in (
            (panel_ref.at[:, pl.ds(offset, span)], span),
            (inv_ref.at[:, pl.ds(offset, span)], span),
            (rhs_ref.at[height - 1], samples),
            (noise_ref.at[height - 1], samples),
        ):
            copies.append(
                pltpu.make_async_copy(source, pack_ref.at[:, pl.ds(at, width)], arrived.at[len(copies)])
            )
            at += width
        offset += span
    for copy in copies:
        copy.start()
    for copy in copies[:2]:
        copy.wait()
    shift = moved_ref[...]
    shift = jnp.where(live_rows(blocks_ref, *shift.shape), shift, jnp.zeros_like(shift))
    boundary = jnp.dot(edge_ref[...], shift, preferred_element_type=jnp.float32)
    pack_ref[:, :samples] = boundary.astype(jnp.bfloat16)
    for copy in copies[2:]:
        copy.wait()


def pair_kernel(own_ref, other_ref, low_ref, top_ref):
    row_count = own_ref.shape[0]
    columns = low_ref.shape[1]
    for start, ref in ((0, own_ref), (row_count, other_ref)):
        low_ref[start : start + row_count, :] = ref[:, :columns]
        top_ref[start : start + row_count, :] = ref[:, columns:]


def join_kernel(column, *refs):
    joined_ref, row = refs[-1], 0
    columns = joined_ref.shape[1]
    for ref in refs[:-1]:
        skipped = 0 if ref.shape[1] == columns else column
        joined_ref[row : row + ref.shape[0], :] = ref[:, skipped : skipped + columns]
        row += ref.shape[0]


def place(pieces, refs, whole_ref, row_count, leaves, first_column):
    columns = whole_ref.shape[1]
    leaf, section = lax.axis_index("leaf"), lax.axis_index("sec")
    for which, start, distances, turned in pieces:
        if isinstance(turned, int):
            owner = section ^ turned
            distance = jnp.where(section == 0, distances[0], distances[1])
        else:
            owner, distance = turned[0], distances[0]
        at = (((leaf ^ distance) & (leaves - 1)) * 2 + owner) * row_count
        ref = refs[which]
        skipped = 0 if ref.shape[1] == columns else first_column
        whole_ref[pl.ds(pl.multiple_of(at, row_count), row_count), :] = ref[
            start : start + row_count, skipped : skipped + columns
        ]


def solve_forward(whole, rows, at, span, samples, children):
    panel = whole[rows, at : at + span]
    inverse = whole[rows, at + span : at + 2 * span]
    rhs = whole[rows, at + 2 * span : at + 2 * span + samples]
    reduced = rhs.astype(jnp.float32) - jnp.dot(panel, children, preferred_element_type=jnp.float32)
    reduced = reduced.astype(jnp.bfloat16)
    return jnp.dot(inverse, reduced, preferred_element_type=jnp.float32).astype(jnp.bfloat16)


def low_kernel(levels, unit, pieces, *refs):
    piece_refs, (whole_ref, *solved_refs) = refs[:-levels], refs[-levels:]
    row_count = unit // 2
    place(pieces, piece_refs, whole_ref, row_count, 2 ** (levels - 1), 0)
    samples = solved_refs[0].shape[1]
    total = whole_ref.shape[0]
    below_ref, at = whole_ref, samples
    for height in range(1, levels):
        span = 2**height * unit
        for group in range(total // span):
            rows = slice(group * span, (group + 1) * span)
            children = below_ref[rows, 0:samples]
            solved_refs[height - 1][rows, :] = solve_forward(whole_ref, rows, at, span, samples, children)
        below_ref = solved_refs[height - 1]
        at += 2 * span + 2 * samples


def leaf_kernel(
    row_count,
    blocks_ref,
    leaf_ref,
    shift_ref,
    noise_ref,
    dev_ref,
    base_ref,
    edge_ref,
    inner_ref,
    scale_ref,
):
    rows, samples = shift_ref.shape
    live = live_rows(blocks_ref, rows, samples)
    shift = shift_ref[...]
    shift = jnp.where(live, shift, jnp.zeros_like(shift))
    zero = jnp.float32(0.0)
    forward = jnp.dot(leaf_ref[...], shift, preferred_element_type=jnp.float32)
    forward = jnp.where(live, forward, zero).astype(jnp.bfloat16)
    summed = forward.astype(jnp.float32) + noise_ref[...].astype(jnp.float32)
    inner = rows - row_count
    edge_ref[...] = summed[inner:, :]
    within = lax.broadcasted_iota(jnp.int32, (rows, samples), 0) < inner
    weight = jnp.where(live & within, summed, zero)
    product = jnp.dot(weight.T.astype(jnp.bfloat16), leaf_ref[...], preferred_element_type=jnp.float32)
    base_ref[...] = product.T
    inner_ref[...] = leaf_ref[inner:, :].astype(jnp.float32).T.astype(jnp.bfloat16)
    for block in range(rows // BLOCK):
        part = slice(block * BLOCK, (block + 1) * BLOCK)
        column = column_of(dev_ref[:, part].astype(jnp.float32))
        scale_ref[part, :] = jnp.where(live[part, :], jnp.broadcast_to(column, (BLOCK, samples)), zero)


def top_kernel(levels, unit, pieces, *refs):
    low_ref, dev_ref, partner_ref, base_ref, edge_ref, inner_ref, scale_ref = refs[:7]
    solved_refs = refs[7 : 7 + levels - 1]
    out_ref, sample_ref, whole_ref, child_ref, x_ref, sum_ref = refs[-6:]
    piece_refs = refs[7 + levels - 1 : -6]
    samples = partner_ref.shape[1]
    row_count = unit // 2
    leaf, section = lax.axis_index("leaf"), lax.axis_index("sec")
    place(pieces, piece_refs, whole_ref, row_count, 2**levels, low_ref.shape[1])
    half = partner_ref.shape[0]
    upper = leaf >> (levels - 1) & 1
    child_ref[pl.ds(pl.multiple_of(upper * half, half), half), :] = solved_refs[-1][...]
    child_ref[pl.ds(pl.multiple_of((1 - upper) * half, half), half), :] = partner_ref[...]
    top_span = 2**levels * unit
    own = solve_forward(whole_ref, slice(0, top_span), 0, top_span, samples, child_ref[...])
    correction = None
    low_at = low_ref.shape[1]
    for height in range(levels, 0, -1):
        span = 2**height * unit
        if height == levels:
            source, at, rows = whole_ref, 0, slice(0, span)
        else:
            low_at -= 2 * span + 2 * samples
            first = ((leaf & (2 ** (levels - 1) - 1)) >> height) * span
            source, at, rows = low_ref, low_at, pl.ds(pl.multiple_of(first, span), span)
            own = solved_refs[height - 1][rows, :]
        noise = source[rows, at + 2 * span + samples : at + 2 * span + 2 * samples]
        summed = (own.astype(jnp.float32) + noise.astype(jnp.float32)).T
        if correction is not None:
            summed = summed - correction
        x = jnp.dot(
            summed.astype(jnp.bfloat16), source[rows, at + span : at + 2 * span], preferred_element_type=jnp.float32
        ).astype(jnp.bfloat16)
        pushed = jnp.dot(x, source[rows, at : at + span], preferred_element_type=jnp.float32)
        x_ref[0:span, :] = x.astype(jnp.float32).T
        mine = pl.ds(pl.multiple_of(((leaf & (2**height - 1)) * 2 + section) * row_count, row_count), row_count)
        scale = column_of(dev_ref[height - 1 : height, :].astype(jnp.float32))
        sample_ref[height - 1] = (scale * x_ref[mine, :]).astype(jnp.bfloat16)
        if height > 1:
            upper = leaf >> (height - 1) & 1
            correction = jnp.where(upper == 1, pushed[:, span // 2 :], pushed[:, : span // 2])
        else:
            sum_ref[...] = pushed.T
            correction = sum_ref[mine, :]
    weight = (edge_ref[...] - correction).astype(jnp.bfloat16)
    back = base_ref[...] + jnp.dot(inner_ref[...], weight, preferred_element_type=jnp.float32)
    out_ref[...] = (scale_ref[...] * back).astype(jnp.bfloat16)


def transposed_dot(matrix, vector):
    return lax.dot_general(matrix, vector, (((0,), (0,)), ((), ())), preferred_element_type=jnp.float32)


def from_partner(block, axis, apart):
    count = lax.axis_size(axis)
    route = []
    for low in range(count):
        high = low | 1 << apart
        if high != low and high < count:
            route += [(low, high), (high, low)]
    return lax.ppermute(block, axis, route)


def pair_gather(block, height):
    leaf_place = lax.axis_index("leaf")
    for bit_index in range(height):
        partner = from_partner(block, "leaf", bit_index)
        upper_half = leaf_place >> bit_index & 1 == 1
        block = jnp.where(
            upper_half, jnp.concatenate([partner, block], 0), jnp.concatenate([block, partner], 0)
        )
    return block


def group_gather(piece, height):
    block = lax.all_gather(piece, "sec", axis=0, tiled=True)
    return pair_gather(block, height)


def halve_pairs(partial_sum, height):
    leaf_place = lax.axis_index("leaf")
    for bit_index in reversed(range(height)):
        half_rows = partial_sum.shape[0] // 2
        lower_rows = partial_sum[:half_rows]
        upper_rows = partial_sum[half_rows:]
        upper_half = leaf_place >> bit_index & 1 == 1
        kept = jnp.where(upper_half, upper_rows, lower_rows)
        outgoing = jnp.where(upper_half, lower_rows, upper_rows)
        partial_sum = kept + from_partner(outgoing, "leaf", bit_index)
    return partial_sum


def group_reduce(partial_sum, height):
    reduced = halve_pairs(partial_sum, height)
    return lax.psum_scatter(reduced, "sec", scatter_dimension=0, tiled=True)


def leafwise_on_device(
    leaf_inv,
    subtree_blocks,
    subtree_shift_rhs,
    leaf_noise,
    leaf_dev,
    sep_inv,
    sep_panel,
    sep_rhs,
    sep_noise,
    sep_dev,
):
    subtree_row_count = leaf_inv.shape[0]
    row_count = sep_inv.shape[0]
    levels = sep_rhs.shape[0]
    sections = lax.axis_size("sec")
    active_rows = subtree_blocks[0, 0] * BLOCK
    row_positions = jnp.arange(subtree_row_count, dtype=jnp.int32)
    row_activity = (row_positions >= subtree_row_count - active_rows)[:, None]
    subtree_shifted = jnp.where(
        row_activity, subtree_shift_rhs, jnp.zeros((), subtree_shift_rhs.dtype)
    )
    forward_subtree = jnp.dot(leaf_inv, subtree_shifted, preferred_element_type=jnp.float32)
    subtree_forward_solution = jnp.where(row_activity, forward_subtree, jnp.float32(0.0)).astype(
        jnp.bfloat16
    )
    top = subtree_forward_solution[subtree_row_count - row_count :]
    solved = []
    for height in range(1, levels + 1):
        span = 2**height * sections * row_count
        offset = (2**height - 2) * sections * row_count
        children = group_gather(top, height)
        panel = sep_panel[:, offset : offset + span]
        inverse_block = sep_inv[:, offset : offset + span]
        reduced = (
            sep_rhs[height - 1].astype(jnp.float32)
            - jnp.dot(panel, children, preferred_element_type=jnp.float32)
        ).astype(jnp.bfloat16)
        whole_reduced = group_gather(reduced, height)
        result = jnp.dot(inverse_block, whole_reduced, preferred_element_type=jnp.float32).astype(
            jnp.bfloat16
        )
        solved.append(result)
        top = result
    samples = [None] * levels
    correction = None
    for height in range(levels, 0, -1):
        span = 2**height * sections * row_count
        offset = (2**height - 2) * sections * row_count
        panel = sep_panel[:, offset : offset + span]
        inverse_block = sep_inv[:, offset : offset + span]
        summed = solved[height - 1].astype(jnp.float32) + sep_noise[height - 1].astype(jnp.float32)
        if correction is not None:
            summed = summed - correction
        vector = summed.astype(jnp.bfloat16)
        backed = group_reduce(transposed_dot(inverse_block, vector), height).astype(
            jnp.bfloat16
        )
        samples[height - 1] = (
            sep_dev[height - 1][:, None].astype(jnp.float32) * backed.astype(jnp.float32)
        ).astype(jnp.bfloat16)
        correction = group_reduce(transposed_dot(panel, backed), height)
    leading = jnp.zeros((subtree_row_count - row_count, correction.shape[1]), jnp.float32)
    placed = jnp.concatenate([leading, correction], axis=0)
    subtree_summed = (
        subtree_forward_solution.astype(jnp.float32) + leaf_noise.astype(jnp.float32) - placed
    )
    subtree_weight = jnp.where(row_activity, subtree_summed, jnp.float32(0.0)).astype(jnp.bfloat16)
    subtree_solution = transposed_dot(leaf_inv, subtree_weight)
    sample_scales = leaf_dev[:, None].astype(jnp.float32)
    subtree_scaled_samples = jnp.where(
        row_activity, sample_scales * subtree_solution, jnp.float32(0.0)
    ).astype(jnp.bfloat16)
    return (subtree_scaled_samples, jnp.stack(samples))


def on_device(
    leaf_inv,
    subtree_blocks,
    subtree_shift_rhs,
    leaf_noise,
    leaf_dev,
    sep_inv,
    sep_panel,
    sep_rhs,
    sep_noise,
    sep_dev,
):
    subtree_rows = leaf_inv.shape[0]
    row_count = sep_inv.shape[0]
    levels, _, samples = sep_rhs.shape
    unit = 2 * row_count
    vmem = pl.BlockSpec(memory_space=pltpu.VMEM)
    short = pl.CostEstimate(flops=1, bytes_accessed=1, transcendentals=0)

    def params(mib):
        return pltpu.CompilerParams(vmem_limit_bytes=mib * 2**20)

    top_columns = 2 * 2**levels * unit + 2 * samples
    low_columns = samples + sum(2 * 2**h * unit + 2 * samples for h in range(1, levels))
    hbm = pl.BlockSpec(memory_space=pltpu.HBM)

    def in_hbm(array):
        return pltpu.with_memory_space_constraint(array, pltpu.HBM)

    blocks = jnp.broadcast_to(subtree_blocks, (8, samples))
    pack = pl.pallas_call(
        functools.partial(pack_kernel, levels),
        out_shape=jax.ShapeDtypeStruct((row_count, low_columns + top_columns), jnp.bfloat16),
        in_specs=[vmem] + [hbm] * 6,
        out_specs=vmem,
        scratch_shapes=[
            pltpu.VMEM((row_count, subtree_rows), jnp.bfloat16),
            pltpu.VMEM((subtree_rows, samples), jnp.bfloat16),
            pltpu.SemaphoreType.DMA((2 + 4 * levels,)),
        ],
        compiler_params=params(4),
        cost_estimate=short,
        name="pack",
    )(blocks, *(in_hbm(x) for x in (leaf_inv, subtree_shift_rhs, sep_panel, sep_inv, sep_rhs, sep_noise)))

    def swap(block):
        return lax.ppermute(block, "sec", [(0, 1), (1, 0)])

    def join(arrays, columns, column, *after):
        rows = sum(array.shape[0] for array in arrays)
        return pl.pallas_call(
            lambda *refs: join_kernel(column, *refs[len(after) :]),
            out_shape=jax.ShapeDtypeStruct((rows, columns), jnp.bfloat16),
            in_specs=[pl.BlockSpec(memory_space=pl.ANY)] * len(after) + [vmem] * len(arrays),
            out_specs=vmem,
            compiler_params=params(4),
            cost_estimate=short,
            name="join",
        )(*after, *arrays)

    pack_other = swap(pack)
    low_pair, top_pair = pl.pallas_call(
        pair_kernel,
        out_shape=(
            jax.ShapeDtypeStruct((unit, low_columns), jnp.bfloat16),
            jax.ShapeDtypeStruct((unit, top_columns), jnp.bfloat16),
        ),
        in_specs=[vmem, vmem],
        out_specs=(vmem, vmem),
        compiler_params=params(4),
        cost_estimate=short,
        name="pair",
    )(pack, pack_other)
    third = to_chips(pack, (3, 3))
    first = to_chips(low_pair, (1, 2))
    both = lax.all_gather(join([third, first], low_columns, 0), "sec", axis=0, tiled=True)
    own = [(pack, 0, (0, 0), 0), (pack_other, 0, (0, 0), 1)]
    quarter = list(own)
    for owner, distance in ((0, 1), (1, 2)):
        row = 3 * row_count * owner
        quarter.append((both, row, (3,), (owner,)))
        quarter.append((both, row + row_count, (distance,), (owner,)))
        quarter.append((both, row + 2 * row_count, (distance,), (1 - owner,)))

    def listed(pieces):
        arrays, places = [], []
        for array, start, distances, turned in pieces:
            if not any(array is known for known in arrays):
                arrays.append(array)
            which = [array is known for known in arrays].index(True)
            places.append((which, start, distances, turned))
        return arrays, places

    arrays, places = listed(quarter)
    quad = 2 ** (levels - 1)
    low_whole, *solved = pl.pallas_call(
        functools.partial(low_kernel, levels, unit, places),
        out_shape=[jax.ShapeDtypeStruct((quad * unit, low_columns), jnp.bfloat16)]
        + [jax.ShapeDtypeStruct((quad * unit, samples), jnp.bfloat16)] * (levels - 1),
        in_specs=[vmem] * len(arrays),
        out_specs=[vmem] * levels,
        compiler_params=params(8),
        cost_estimate=short,
        name="low",
    )(*arrays)
    partner = to_chips(solved[-1], (quad, quad))

    trips = [(pack, (3, 3)), (top_pair, (1, 2)), (top_pair, (4, 5)), (top_pair, (6, 7))]
    arrived = [third] + [to_chips(block, distances) for block, distances in trips[1:]]
    here = join(arrived, top_columns, low_columns, solved[-1])
    there = swap(here)
    far = own
    row = 0
    for block, (first, second) in trips:
        for turned in range(block.shape[0] // row_count):
            far.append((here, row, (first, second), turned))
            far.append((there, row, (second, first), 1 - turned))
            row += row_count

    base, edge, inner, scale = pl.pallas_call(
        functools.partial(leaf_kernel, row_count),
        out_shape=(
            jax.ShapeDtypeStruct((subtree_rows, samples), jnp.float32),
            jax.ShapeDtypeStruct((row_count, samples), jnp.float32),
            jax.ShapeDtypeStruct((subtree_rows, row_count), jnp.bfloat16),
            jax.ShapeDtypeStruct((subtree_rows, samples), jnp.float32),
        ),
        in_specs=[vmem] * 5,
        out_specs=(vmem,) * 4,
        compiler_params=params(12),
        cost_estimate=short,
        name="leaf",
    )(blocks, leaf_inv, subtree_shift_rhs, leaf_noise, leaf_dev[None, :])

    arrays, places = listed(far)
    span = 2**levels * unit
    return pl.pallas_call(
        functools.partial(top_kernel, levels, unit, places),
        out_shape=(
            jax.ShapeDtypeStruct((subtree_rows, samples), jnp.bfloat16),
            jax.ShapeDtypeStruct((levels, row_count, samples), jnp.bfloat16),
        ),
        in_specs=[vmem] * (7 + levels - 1 + len(arrays)),
        out_specs=(vmem, vmem),
        scratch_shapes=[
            pltpu.VMEM((span, top_columns), jnp.bfloat16),
            pltpu.VMEM((span, samples), jnp.bfloat16),
            pltpu.VMEM((span, samples), jnp.float32),
            pltpu.VMEM((unit * 2, samples), jnp.float32),
        ],
        compiler_params=params(16),
        name="top",
    )(low_whole, sep_dev, partner, base, edge, inner, scale, *solved, *arrays)


def solution(mesh):
    rows = P(AXES, None)
    in_specs = (
        rows,
        P("leaf", "sec"),
        rows,
        rows,
        P(AXES),
        rows,
        rows,
        P(None, AXES, None),
        P(None, AXES, None),
        P(None, AXES),
    )
    out_specs = (rows, P(None, AXES, None))

    def program(*arrays):
        levels = arrays[7].shape[0]
        paired = levels == 3 and mesh.shape["sec"] == 2 and mesh.shape["leaf"] % 2**levels == 0
        return on_device(*arrays) if paired else leafwise_on_device(*arrays)

    return jax.shard_map(program, mesh=mesh, in_specs=in_specs, out_specs=out_specs, check_vma=False)
```

```python
import functools

import jax
import jax.numpy as jnp
from jax import lax
from jax.experimental import pallas as pl
from jax.experimental.pallas import tpu as pltpu
from jax.sharding import PartitionSpec as P

BLOCK = 128
AXES = ("leaf", "sec")


def to_chips(block, distances):
    leaves, sections = lax.axis_size("leaf"), lax.axis_size("sec")
    route = []
    for leaf in range(leaves):
        for section, distance in enumerate(distances):
            route.append((leaf * sections + section, (leaf ^ distance) * sections + section))
    return lax.ppermute(block, AXES, route)


def column_of(row):
    count = row.shape[1]
    across = lax.broadcasted_iota(jnp.int32, (count, count), 1)
    down = lax.broadcasted_iota(jnp.int32, (count, count), 0)
    return jnp.sum(jnp.where(across == down, row, jnp.zeros_like(row)), axis=1, keepdims=True)


def live_rows(dead_ref, rows, columns):
    live_from = dead_ref[0:1, 0:columns]
    return lax.broadcasted_iota(jnp.int32, (rows, columns), 0) >= live_from


def pack_kernel(
    levels,
    dead_ref,
    leaf_ref,
    shift_ref,
    panel_ref,
    inv_ref,
    rhs_ref,
    noise_ref,
    low_ref,
    top_ref,
    edge_ref,
    moved_ref,
    arrived,
):
    row_count, samples = edge_ref.shape[0], shift_ref.shape[1]
    subtree_rows = shift_ref.shape[0]
    copies = [
        pltpu.make_async_copy(shift_ref, moved_ref, arrived.at[0]),
        pltpu.make_async_copy(leaf_ref.at[pl.ds(subtree_rows - row_count, row_count)], edge_ref, arrived.at[1]),
    ]
    at, offset = samples, 0
    unit = panel_ref.shape[1] // (2 ** (levels + 1) - 2)
    for height in range(1, levels + 1):
        span = 2**height * unit
        out = low_ref if height < levels else top_ref
        at = at if height < levels else 0
        for source, width in (
            (panel_ref.at[:, pl.ds(offset, span)], span),
            (inv_ref.at[:, pl.ds(offset, span)], span),
            (rhs_ref.at[height - 1], samples),
            (noise_ref.at[height - 1], samples),
        ):
            copies.append(
                pltpu.make_async_copy(source, out.at[:, pl.ds(at, width)], arrived.at[len(copies)])
            )
            at += width
        offset += span
    for copy in copies:
        copy.start()
    for copy in copies[:2]:
        copy.wait()
    shift = moved_ref[...]
    shift = jnp.where(live_rows(dead_ref, *shift.shape), shift, jnp.zeros_like(shift))
    boundary = jnp.dot(edge_ref[...], shift, preferred_element_type=jnp.float32)
    low_ref[:, :samples] = boundary.astype(jnp.bfloat16)
    for copy in copies[2:]:
        copy.wait()


def join_kernel(*refs):
    joined_ref, row = refs[-1], 0
    for ref in refs[:-1]:
        joined_ref[row : row + ref.shape[0], :] = ref[...]
        row += ref.shape[0]


def place(pieces, refs, whole_ref, row_count, leaves):
    leaf, section = lax.axis_index("leaf"), lax.axis_index("sec")
    for which, start, distances, turned in pieces:
        if isinstance(turned, int):
            owner = section ^ turned
            distance = jnp.where(section == 0, distances[0], distances[1])
        else:
            owner, distance = turned[0], distances[0]
        at = (((leaf ^ distance) & (leaves - 1)) * 2 + owner) * row_count
        ref = refs[which]
        whole_ref[pl.ds(pl.multiple_of(at, row_count), row_count), :] = ref[start : start + row_count, :]


def solve_forward(whole, rows, at, span, samples, children):
    panel = whole[rows, at : at + span]
    inverse = whole[rows, at + span : at + 2 * span]
    rhs = whole[rows, at + 2 * span : at + 2 * span + samples]
    reduced = rhs.astype(jnp.float32) - jnp.dot(panel, children, preferred_element_type=jnp.float32)
    reduced = reduced.astype(jnp.bfloat16)
    return jnp.dot(inverse, reduced, preferred_element_type=jnp.float32).astype(jnp.bfloat16)


def low_kernel(levels, unit, pieces, *refs):
    piece_refs, (whole_ref, *solved_refs) = refs[:-levels], refs[-levels:]
    row_count = unit // 2
    place(pieces, piece_refs, whole_ref, row_count, 2 ** (levels - 1))
    samples = solved_refs[0].shape[1]
    total = whole_ref.shape[0]
    below_ref, at = whole_ref, samples
    for height in range(1, levels):
        span = 2**height * unit
        for group in range(total // span):
            rows = slice(group * span, (group + 1) * span)
            children = below_ref[rows, 0:samples]
            solved_refs[height - 1][rows, :] = solve_forward(whole_ref, rows, at, span, samples, children)
        below_ref = solved_refs[height - 1]
        at += 2 * span + 2 * samples


def leaf_kernel(
    row_count,
    dead_ref,
    leaf_ref,
    shift_ref,
    noise_ref,
    dev_ref,
    base_ref,
    edge_ref,
    inner_ref,
    scale_ref,
):
    rows, samples = shift_ref.shape
    live = live_rows(dead_ref, rows, samples)
    shift = shift_ref[...]
    shift = jnp.where(live, shift, jnp.zeros_like(shift))
    zero = jnp.float32(0.0)
    forward = jnp.dot(leaf_ref[...], shift, preferred_element_type=jnp.float32)
    forward = jnp.where(live, forward, zero).astype(jnp.bfloat16)
    summed = forward.astype(jnp.float32) + noise_ref[...].astype(jnp.float32)
    inner = rows - row_count
    edge_ref[...] = summed[inner:, :]
    within = lax.broadcasted_iota(jnp.int32, (rows, samples), 0) < inner
    weight = jnp.where(live & within, summed, zero)
    product = jnp.dot(weight.T.astype(jnp.bfloat16), leaf_ref[...], preferred_element_type=jnp.float32)
    base_ref[...] = product.T
    inner_ref[...] = leaf_ref[inner:, :].astype(jnp.float32).T.astype(jnp.bfloat16)
    for block in range(rows // BLOCK):
        part = slice(block * BLOCK, (block + 1) * BLOCK)
        column = column_of(dev_ref[:, part].astype(jnp.float32))
        scale_ref[part, :] = jnp.where(live[part, :], jnp.broadcast_to(column, (BLOCK, samples)), zero)


def top_kernel(levels, unit, pieces, *refs):
    low_ref, dev_ref, partner_ref, base_ref, edge_ref, inner_ref, scale_ref = refs[:7]
    solved_refs = refs[7 : 7 + levels - 1]
    out_ref, sample_ref, whole_ref, child_ref, x_ref, sum_ref = refs[-6:]
    piece_refs = refs[7 + levels - 1 : -6]
    samples = partner_ref.shape[1]
    row_count = unit // 2
    leaf, section = lax.axis_index("leaf"), lax.axis_index("sec")
    place(pieces, piece_refs, whole_ref, row_count, 2**levels)
    half = partner_ref.shape[0]
    upper = leaf >> (levels - 1) & 1
    child_ref[pl.ds(pl.multiple_of(upper * half, half), half), :] = solved_refs[-1][...]
    child_ref[pl.ds(pl.multiple_of((1 - upper) * half, half), half), :] = partner_ref[...]
    top_span = 2**levels * unit
    own = solve_forward(whole_ref, slice(0, top_span), 0, top_span, samples, child_ref[...])
    correction = None
    low_at = low_ref.shape[1]
    for height in range(levels, 0, -1):
        span = 2**height * unit
        if height == levels:
            source, at, rows = whole_ref, 0, slice(0, span)
        else:
            low_at -= 2 * span + 2 * samples
            first = ((leaf & (2 ** (levels - 1) - 1)) >> height) * span
            source, at, rows = low_ref, low_at, pl.ds(pl.multiple_of(first, span), span)
            own = solved_refs[height - 1][rows, :]
        noise = source[rows, at + 2 * span + samples : at + 2 * span + 2 * samples]
        summed = (own.astype(jnp.float32) + noise.astype(jnp.float32)).T
        if correction is not None:
            summed = summed - correction
        x = jnp.dot(
            summed.astype(jnp.bfloat16), source[rows, at + span : at + 2 * span], preferred_element_type=jnp.float32
        ).astype(jnp.bfloat16)
        pushed = jnp.dot(x, source[rows, at : at + span], preferred_element_type=jnp.float32)
        x_ref[0:span, :] = x.astype(jnp.float32).T
        mine = pl.ds(pl.multiple_of(((leaf & (2**height - 1)) * 2 + section) * row_count, row_count), row_count)
        scale = column_of(dev_ref[height - 1 : height, :].astype(jnp.float32))
        sample_ref[height - 1] = (scale * x_ref[mine, :]).astype(jnp.bfloat16)
        if height > 1:
            upper = leaf >> (height - 1) & 1
            correction = jnp.where(upper == 1, pushed[:, span // 2 :], pushed[:, : span // 2])
        else:
            sum_ref[...] = pushed.T
            correction = sum_ref[mine, :]
    weight = (edge_ref[...] - correction).astype(jnp.bfloat16)
    back = base_ref[...] + jnp.dot(inner_ref[...], weight, preferred_element_type=jnp.float32)
    out_ref[...] = (scale_ref[...] * back).astype(jnp.bfloat16)


def transposed_dot(matrix, vector):
    return lax.dot_general(matrix, vector, (((0,), (0,)), ((), ())), preferred_element_type=jnp.float32)


def from_partner(block, axis, apart):
    count = lax.axis_size(axis)
    route = []
    for low in range(count):
        high = low | 1 << apart
        if high != low and high < count:
            route += [(low, high), (high, low)]
    return lax.ppermute(block, axis, route)


def pair_gather(block, height):
    leaf_place = lax.axis_index("leaf")
    for bit_index in range(height):
        partner = from_partner(block, "leaf", bit_index)
        upper_half = leaf_place >> bit_index & 1 == 1
        block = jnp.where(
            upper_half, jnp.concatenate([partner, block], 0), jnp.concatenate([block, partner], 0)
        )
    return block


def group_gather(piece, height):
    block = lax.all_gather(piece, "sec", axis=0, tiled=True)
    return pair_gather(block, height)


def halve_pairs(partial_sum, height):
    leaf_place = lax.axis_index("leaf")
    for bit_index in reversed(range(height)):
        half_rows = partial_sum.shape[0] // 2
        lower_rows = partial_sum[:half_rows]
        upper_rows = partial_sum[half_rows:]
        upper_half = leaf_place >> bit_index & 1 == 1
        kept = jnp.where(upper_half, upper_rows, lower_rows)
        outgoing = jnp.where(upper_half, lower_rows, upper_rows)
        partial_sum = kept + from_partner(outgoing, "leaf", bit_index)
    return partial_sum


def group_reduce(partial_sum, height):
    reduced = halve_pairs(partial_sum, height)
    return lax.psum_scatter(reduced, "sec", scatter_dimension=0, tiled=True)


def leafwise_on_device(
    leaf_inv,
    subtree_blocks,
    subtree_shift_rhs,
    leaf_noise,
    leaf_dev,
    sep_inv,
    sep_panel,
    sep_rhs,
    sep_noise,
    sep_dev,
):
    subtree_row_count = leaf_inv.shape[0]
    row_count = sep_inv.shape[0]
    levels = sep_rhs.shape[0]
    sections = lax.axis_size("sec")
    active_rows = subtree_blocks[0, 0] * BLOCK
    row_positions = jnp.arange(subtree_row_count, dtype=jnp.int32)
    row_activity = (row_positions >= subtree_row_count - active_rows)[:, None]
    subtree_shifted = jnp.where(
        row_activity, subtree_shift_rhs, jnp.zeros((), subtree_shift_rhs.dtype)
    )
    forward_subtree = jnp.dot(leaf_inv, subtree_shifted, preferred_element_type=jnp.float32)
    subtree_forward_solution = jnp.where(row_activity, forward_subtree, jnp.float32(0.0)).astype(
        jnp.bfloat16
    )
    top = subtree_forward_solution[subtree_row_count - row_count :]
    solved = []
    for height in range(1, levels + 1):
        span = 2**height * sections * row_count
        offset = (2**height - 2) * sections * row_count
        children = group_gather(top, height)
        panel = sep_panel[:, offset : offset + span]
        inverse_block = sep_inv[:, offset : offset + span]
        reduced = (
            sep_rhs[height - 1].astype(jnp.float32)
            - jnp.dot(panel, children, preferred_element_type=jnp.float32)
        ).astype(jnp.bfloat16)
        whole_reduced = group_gather(reduced, height)
        result = jnp.dot(inverse_block, whole_reduced, preferred_element_type=jnp.float32).astype(
            jnp.bfloat16
        )
        solved.append(result)
        top = result
    samples = [None] * levels
    correction = None
    for height in range(levels, 0, -1):
        span = 2**height * sections * row_count
        offset = (2**height - 2) * sections * row_count
        panel = sep_panel[:, offset : offset + span]
        inverse_block = sep_inv[:, offset : offset + span]
        summed = solved[height - 1].astype(jnp.float32) + sep_noise[height - 1].astype(jnp.float32)
        if correction is not None:
            summed = summed - correction
        vector = summed.astype(jnp.bfloat16)
        backed = group_reduce(transposed_dot(inverse_block, vector), height).astype(
            jnp.bfloat16
        )
        samples[height - 1] = (
            sep_dev[height - 1][:, None].astype(jnp.float32) * backed.astype(jnp.float32)
        ).astype(jnp.bfloat16)
        correction = group_reduce(transposed_dot(panel, backed), height)
    leading = jnp.zeros((subtree_row_count - row_count, correction.shape[1]), jnp.float32)
    placed = jnp.concatenate([leading, correction], axis=0)
    subtree_summed = (
        subtree_forward_solution.astype(jnp.float32) + leaf_noise.astype(jnp.float32) - placed
    )
    subtree_weight = jnp.where(row_activity, subtree_summed, jnp.float32(0.0)).astype(jnp.bfloat16)
    subtree_solution = transposed_dot(leaf_inv, subtree_weight)
    sample_scales = leaf_dev[:, None].astype(jnp.float32)
    subtree_scaled_samples = jnp.where(
        row_activity, sample_scales * subtree_solution, jnp.float32(0.0)
    ).astype(jnp.bfloat16)
    return (subtree_scaled_samples, jnp.stack(samples))


def on_device(
    leaf_inv,
    subtree_blocks,
    subtree_shift_rhs,
    leaf_noise,
    leaf_dev,
    sep_inv,
    sep_panel,
    sep_rhs,
    sep_noise,
    sep_dev,
):
    subtree_rows = leaf_inv.shape[0]
    row_count = sep_inv.shape[0]
    levels, _, samples = sep_rhs.shape
    unit = 2 * row_count
    vmem = pl.BlockSpec(memory_space=pltpu.VMEM)

    def params(mib):
        return pltpu.CompilerParams(vmem_limit_bytes=mib * 2**20)

    top_columns = 2 * 2**levels * unit + 2 * samples
    low_columns = samples + sum(2 * 2**h * unit + 2 * samples for h in range(1, levels))
    hbm = pl.BlockSpec(memory_space=pltpu.HBM)

    def in_hbm(array):
        return pltpu.with_memory_space_constraint(array, pltpu.HBM)

    dead = jnp.full((8, samples), subtree_rows - subtree_blocks[0, 0] * BLOCK, jnp.int32)
    low, top = pl.pallas_call(
        functools.partial(pack_kernel, levels),
        out_shape=(
            jax.ShapeDtypeStruct((row_count, low_columns), jnp.bfloat16),
            jax.ShapeDtypeStruct((row_count, top_columns), jnp.bfloat16),
        ),
        in_specs=[vmem] + [hbm] * 6,
        out_specs=(vmem, vmem),
        scratch_shapes=[
            pltpu.VMEM((row_count, subtree_rows), jnp.bfloat16),
            pltpu.VMEM((subtree_rows, samples), jnp.bfloat16),
            pltpu.SemaphoreType.DMA((2 + 4 * levels,)),
        ],
        compiler_params=params(4),
        name="pack",
    )(dead, *(in_hbm(x) for x in (leaf_inv, subtree_shift_rhs, sep_panel, sep_inv, sep_rhs, sep_noise)))

    def swap(block):
        return lax.ppermute(block, "sec", [(0, 1), (1, 0)])

    def join(arrays, *after, flops=0):
        rows = sum(array.shape[0] for array in arrays)
        return pl.pallas_call(
            lambda *refs: join_kernel(*refs[len(after) :]),
            out_shape=jax.ShapeDtypeStruct((rows, arrays[0].shape[1]), arrays[0].dtype),
            in_specs=[pl.BlockSpec(memory_space=pl.ANY)] * len(after) + [vmem] * len(arrays),
            out_specs=vmem,
            compiler_params=params(4),
            cost_estimate=pl.CostEstimate(flops=flops, bytes_accessed=0, transcendentals=0) if flops else None,
            name="join",
        )(*after, *arrays)

    quad = 2 ** (levels - 1)
    near = join([low] + [to_chips(low, (distance, distance)) for distance in range(1, quad)])
    near = lax.all_gather(near, "sec", axis=0, tiled=True)
    quarter = []
    for owner in range(2):
        for distance in range(quad):
            quarter.append((near, (owner * quad + distance) * row_count, (distance,), (owner,)))

    top_other = swap(top)
    top_pair = join([top, top_other])

    def listed(pieces):
        arrays, places = [], []
        for array, start, distances, turned in pieces:
            if not any(array is known for known in arrays):
                arrays.append(array)
            which = [array is known for known in arrays].index(True)
            places.append((which, start, distances, turned))
        return arrays, places

    arrays, places = listed(quarter)
    low_whole, *solved = pl.pallas_call(
        functools.partial(low_kernel, levels, unit, places),
        out_shape=[jax.ShapeDtypeStruct((quad * unit, low_columns), jnp.bfloat16)]
        + [jax.ShapeDtypeStruct((quad * unit, samples), jnp.bfloat16)] * (levels - 1),
        in_specs=[vmem] * len(arrays),
        out_specs=[vmem] * levels,
        compiler_params=params(8),
        name="low",
    )(*arrays)
    partner = to_chips(solved[-1], (quad, quad))

    trips = [(top, (3, 3)), (top_pair, (1, 2)), (top_pair, (4, 5)), (top_pair, (6, 7))]
    here = join([to_chips(block, distances) for block, distances in trips], solved[-1])
    there = swap(here)
    far = [(top, 0, (0, 0), 0), (top_other, 0, (0, 0), 1)]
    row = 0
    for block, (first, second) in trips:
        for turned in range(block.shape[0] // row_count):
            far.append((here, row, (first, second), turned))
            far.append((there, row, (second, first), 1 - turned))
            row += row_count

    base, edge, inner, scale = pl.pallas_call(
        functools.partial(leaf_kernel, row_count),
        out_shape=(
            jax.ShapeDtypeStruct((subtree_rows, samples), jnp.float32),
            jax.ShapeDtypeStruct((row_count, samples), jnp.float32),
            jax.ShapeDtypeStruct((subtree_rows, row_count), jnp.bfloat16),
            jax.ShapeDtypeStruct((subtree_rows, samples), jnp.float32),
        ),
        in_specs=[vmem] * 5,
        out_specs=(vmem,) * 4,
        compiler_params=params(12),
        name="leaf",
    )(dead, leaf_inv, subtree_shift_rhs, leaf_noise, leaf_dev[None, :])

    edge = join([edge], partner, flops=10**10)
    arrays, places = listed(far)
    span = 2**levels * unit
    return pl.pallas_call(
        functools.partial(top_kernel, levels, unit, places),
        out_shape=(
            jax.ShapeDtypeStruct((subtree_rows, samples), jnp.bfloat16),
            jax.ShapeDtypeStruct((levels, row_count, samples), jnp.bfloat16),
        ),
        in_specs=[vmem] * (7 + levels - 1 + len(arrays)),
        out_specs=(vmem, vmem),
        scratch_shapes=[
            pltpu.VMEM((span, top_columns), jnp.bfloat16),
            pltpu.VMEM((span, samples), jnp.bfloat16),
            pltpu.VMEM((span, samples), jnp.float32),
            pltpu.VMEM((unit * 2, samples), jnp.float32),
        ],
        compiler_params=params(16),
        name="top",
    )(low_whole, sep_dev, partner, base, edge, inner, scale, *solved, *arrays)


def solution(mesh):
    rows = P(AXES, None)
    in_specs = (
        rows,
        P("leaf", "sec"),
        rows,
        rows,
        P(AXES),
        rows,
        rows,
        P(None, AXES, None),
        P(None, AXES, None),
        P(None, AXES),
    )
    out_specs = (rows, P(None, AXES, None))

    def program(*arrays):
        levels = arrays[7].shape[0]
        paired = levels == 3 and mesh.shape["sec"] == 2 and mesh.shape["leaf"] % 2**levels == 0
        return on_device(*arrays) if paired else leafwise_on_device(*arrays)

    return jax.shard_map(program, mesh=mesh, in_specs=in_specs, out_specs=out_specs, check_vma=False)
```

```python
import functools

import jax
import jax.numpy as jnp
from jax import lax
from jax.experimental import pallas as pl
from jax.experimental.pallas import tpu as pltpu
from jax.sharding import PartitionSpec as P

BLOCK = 128
AXES = ("leaf", "sec")


def to_chips(block, distances):
    leaves, sections = lax.axis_size("leaf"), lax.axis_size("sec")
    route = []
    for leaf in range(leaves):
        for section, distance in enumerate(distances):
            route.append((leaf * sections + section, (leaf ^ distance) * sections + section))
    return lax.ppermute(block, AXES, route)


def column_of(row):
    count = row.shape[1]
    across = lax.broadcasted_iota(jnp.int32, (count, count), 1)
    down = lax.broadcasted_iota(jnp.int32, (count, count), 0)
    return jnp.sum(jnp.where(across == down, row, jnp.zeros_like(row)), axis=1, keepdims=True)


def live_rows(blocks_ref, shape, dimension):
    return lax.broadcasted_iota(jnp.int32, shape, dimension) >= shape[dimension] - blocks_ref[0, 0] * BLOCK


def pack_kernel(levels, blocks_ref, *refs):
    sources, (low_ref, top_ref), moved, arrived = refs[:6], refs[6:8], refs[8:14], refs[14]
    rows = sources[0].shape[0]
    row_count = moved[0].shape[0]
    parts = (sources[0].at[pl.ds(rows - row_count, row_count)],) + sources[1:]
    copies = [pltpu.make_async_copy(part, ref, arrived.at[n]) for n, (part, ref) in enumerate(zip(parts, moved))]
    for copy in copies:
        copy.start()
    edge_ref, shift_ref, panel_ref, inv_ref, rhs_ref, noise_ref = moved
    samples = shift_ref.shape[1]
    for copy in copies[2:]:
        copy.wait()
    unit = panel_ref.shape[1] // (2 ** (levels + 1) - 2)
    at, offset = samples, 0
    for height in range(1, levels + 1):
        span = 2**height * unit
        out = low_ref if height < levels else top_ref
        at = at if height < levels else 0
        out[:, at : at + span] = panel_ref[:, offset : offset + span]
        out[:, at + span : at + 2 * span] = inv_ref[:, offset : offset + span]
        out[:, at + 2 * span : at + 2 * span + samples] = rhs_ref[height - 1]
        out[:, at + 2 * span + samples : at + 2 * span + 2 * samples] = noise_ref[height - 1]
        at += 2 * span + 2 * samples
        offset += span
    for copy in copies[:2]:
        copy.wait()
    inverse = edge_ref[...]
    inverse = jnp.where(live_rows(blocks_ref, inverse.shape, 1), inverse, jnp.zeros_like(inverse))
    boundary = jnp.dot(inverse, shift_ref[...], preferred_element_type=jnp.float32)
    low_ref[:, :samples] = boundary.astype(jnp.bfloat16)


def join_kernel(*refs):
    joined_ref, row = refs[-1], 0
    for ref in refs[:-1]:
        joined_ref[row : row + ref.shape[0], :] = ref[...]
        row += ref.shape[0]


def place(pieces, refs, whole_ref, row_count, leaves):
    leaf, section = lax.axis_index("leaf"), lax.axis_index("sec")
    for which, start, distances, turned in pieces:
        if isinstance(turned, int):
            owner = section ^ turned
            distance = jnp.where(section == 0, distances[0], distances[1])
        else:
            owner, distance = turned[0], distances[0]
        at = (((leaf ^ distance) & (leaves - 1)) * 2 + owner) * row_count
        ref = refs[which]
        whole_ref[pl.ds(pl.multiple_of(at, row_count), row_count), :] = ref[start : start + row_count, :]


def solve_forward(whole, rows, at, span, samples, children):
    panel = whole[rows, at : at + span]
    inverse = whole[rows, at + span : at + 2 * span]
    rhs = whole[rows, at + 2 * span : at + 2 * span + samples]
    reduced = rhs.astype(jnp.float32) - jnp.dot(panel, children, preferred_element_type=jnp.float32)
    reduced = reduced.astype(jnp.bfloat16)
    return jnp.dot(inverse, reduced, preferred_element_type=jnp.float32).astype(jnp.bfloat16)


def low_kernel(levels, unit, pieces, *refs):
    piece_refs, (whole_ref, *solved_refs) = refs[: -levels - 1], refs[-levels:]
    row_count = unit // 2
    place(pieces, piece_refs, whole_ref, row_count, 2 ** (levels - 1))
    samples = solved_refs[0].shape[1]
    total = whole_ref.shape[0]
    below_ref, at = whole_ref, samples
    for height in range(1, levels):
        span = 2**height * unit
        for group in range(total // span):
            rows = slice(group * span, (group + 1) * span)
            children = below_ref[rows, 0:samples]
            solved_refs[height - 1][rows, :] = solve_forward(whole_ref, rows, at, span, samples, children)
        below_ref = solved_refs[height - 1]
        at += 2 * span + 2 * samples


def leaf_kernel(
    row_count,
    blocks_ref,
    leaf_ref,
    shift_ref,
    noise_ref,
    dev_ref,
    sep_dev_ref,
    base_ref,
    edge_ref,
    inner_ref,
    scale_ref,
    sep_scale_ref,
):
    rows, samples = shift_ref.shape
    live = live_rows(blocks_ref, (rows, samples), 0)
    shift = shift_ref[...]
    shift = jnp.where(live, shift, jnp.zeros_like(shift))
    zero = jnp.float32(0.0)
    forward = jnp.dot(leaf_ref[...], shift, preferred_element_type=jnp.float32)
    forward = jnp.where(live, forward, zero).astype(jnp.bfloat16)
    summed = forward.astype(jnp.float32) + noise_ref[...].astype(jnp.float32)
    inner = rows - row_count
    edge_ref[...] = summed[inner:, :]
    within = lax.broadcasted_iota(jnp.int32, (rows, samples), 0) < inner
    weight = jnp.where(live & within, summed, zero)
    product = jnp.dot(weight.T.astype(jnp.bfloat16), leaf_ref[...], preferred_element_type=jnp.float32)
    base_ref[...] = product.T
    inner_ref[...] = leaf_ref[inner:, :].astype(jnp.float32).T.astype(jnp.bfloat16)
    for block in range(rows // BLOCK):
        part = slice(block * BLOCK, (block + 1) * BLOCK)
        column = column_of(dev_ref[:, part].astype(jnp.float32))
        scale_ref[part, :] = jnp.where(live[part, :], jnp.broadcast_to(column, (BLOCK, samples)), zero)
    for height in range(sep_scale_ref.shape[0]):
        column = column_of(sep_dev_ref[height : height + 1, :].astype(jnp.float32))
        sep_scale_ref[height] = jnp.broadcast_to(column, (row_count, samples))


def top_kernel(levels, unit, pieces, *refs):
    low_ref, sep_scale_ref, partner_ref, base_ref, edge_ref, inner_ref, scale_ref = refs[:7]
    solved_refs = refs[7 : 7 + levels - 1]
    out_ref, sample_ref, whole_ref, child_ref, x_ref, sum_ref = refs[-6:]
    piece_refs = refs[7 + levels - 1 : -6]
    samples = partner_ref.shape[1]
    row_count = unit // 2
    leaf, section = lax.axis_index("leaf"), lax.axis_index("sec")
    place(pieces, piece_refs, whole_ref, row_count, 2**levels)
    half = partner_ref.shape[0]
    upper = leaf >> (levels - 1) & 1
    child_ref[pl.ds(pl.multiple_of(upper * half, half), half), :] = solved_refs[-1][...]
    child_ref[pl.ds(pl.multiple_of((1 - upper) * half, half), half), :] = partner_ref[...]
    top_span = 2**levels * unit
    own = solve_forward(whole_ref, slice(0, top_span), 0, top_span, samples, child_ref[...])
    correction = None
    low_at = low_ref.shape[1]
    for height in range(levels, 0, -1):
        span = 2**height * unit
        if height == levels:
            source, at, rows = whole_ref, 0, slice(0, span)
        else:
            low_at -= 2 * span + 2 * samples
            first = ((leaf & (2 ** (levels - 1) - 1)) >> height) * span
            source, at, rows = low_ref, low_at, pl.ds(pl.multiple_of(first, span), span)
            own = solved_refs[height - 1][rows, :]
        noise = source[rows, at + 2 * span + samples : at + 2 * span + 2 * samples]
        summed = (own.astype(jnp.float32) + noise.astype(jnp.float32)).T
        if correction is not None:
            summed = summed - correction
        x = jnp.dot(
            summed.astype(jnp.bfloat16), source[rows, at + span : at + 2 * span], preferred_element_type=jnp.float32
        ).astype(jnp.bfloat16)
        pushed = jnp.dot(x, source[rows, at : at + span], preferred_element_type=jnp.float32)
        x_ref[0:span, :] = x.astype(jnp.float32).T
        mine = pl.ds(pl.multiple_of(((leaf & (2**height - 1)) * 2 + section) * row_count, row_count), row_count)
        sample_ref[height - 1] = (sep_scale_ref[height - 1] * x_ref[mine, :]).astype(jnp.bfloat16)
        if height > 1:
            upper = leaf >> (height - 1) & 1
            correction = jnp.where(upper == 1, pushed[:, span // 2 :], pushed[:, : span // 2])
        else:
            sum_ref[...] = pushed.T
            correction = sum_ref[mine, :]
    weight = (edge_ref[...] - correction).astype(jnp.bfloat16)
    back = base_ref[...] + jnp.dot(inner_ref[...], weight, preferred_element_type=jnp.float32)
    out_ref[...] = (scale_ref[...] * back).astype(jnp.bfloat16)


def transposed_dot(matrix, vector):
    return lax.dot_general(matrix, vector, (((0,), (0,)), ((), ())), preferred_element_type=jnp.float32)


def from_partner(block, axis, apart):
    count = lax.axis_size(axis)
    route = []
    for low in range(count):
        high = low | 1 << apart
        if high != low and high < count:
            route += [(low, high), (high, low)]
    return lax.ppermute(block, axis, route)


def pair_gather(block, height):
    leaf_place = lax.axis_index("leaf")
    for bit_index in range(height):
        partner = from_partner(block, "leaf", bit_index)
        upper_half = leaf_place >> bit_index & 1 == 1
        block = jnp.where(
            upper_half, jnp.concatenate([partner, block], 0), jnp.concatenate([block, partner], 0)
        )
    return block


def group_gather(piece, height):
    block = lax.all_gather(piece, "sec", axis=0, tiled=True)
    return pair_gather(block, height)


def halve_pairs(partial_sum, height):
    leaf_place = lax.axis_index("leaf")
    for bit_index in reversed(range(height)):
        half_rows = partial_sum.shape[0] // 2
        lower_rows = partial_sum[:half_rows]
        upper_rows = partial_sum[half_rows:]
        upper_half = leaf_place >> bit_index & 1 == 1
        kept = jnp.where(upper_half, upper_rows, lower_rows)
        outgoing = jnp.where(upper_half, lower_rows, upper_rows)
        partial_sum = kept + from_partner(outgoing, "leaf", bit_index)
    return partial_sum


def group_reduce(partial_sum, height):
    reduced = halve_pairs(partial_sum, height)
    return lax.psum_scatter(reduced, "sec", scatter_dimension=0, tiled=True)


def leafwise_on_device(
    leaf_inv,
    subtree_blocks,
    subtree_shift_rhs,
    leaf_noise,
    leaf_dev,
    sep_inv,
    sep_panel,
    sep_rhs,
    sep_noise,
    sep_dev,
):
    subtree_row_count = leaf_inv.shape[0]
    row_count = sep_inv.shape[0]
    levels = sep_rhs.shape[0]
    sections = lax.axis_size("sec")
    active_rows = subtree_blocks[0, 0] * BLOCK
    row_positions = jnp.arange(subtree_row_count, dtype=jnp.int32)
    row_activity = (row_positions >= subtree_row_count - active_rows)[:, None]
    subtree_shifted = jnp.where(
        row_activity, subtree_shift_rhs, jnp.zeros((), subtree_shift_rhs.dtype)
    )
    forward_subtree = jnp.dot(leaf_inv, subtree_shifted, preferred_element_type=jnp.float32)
    subtree_forward_solution = jnp.where(row_activity, forward_subtree, jnp.float32(0.0)).astype(
        jnp.bfloat16
    )
    top = subtree_forward_solution[subtree_row_count - row_count :]
    solved = []
    for height in range(1, levels + 1):
        span = 2**height * sections * row_count
        offset = (2**height - 2) * sections * row_count
        children = group_gather(top, height)
        panel = sep_panel[:, offset : offset + span]
        inverse_block = sep_inv[:, offset : offset + span]
        reduced = (
            sep_rhs[height - 1].astype(jnp.float32)
            - jnp.dot(panel, children, preferred_element_type=jnp.float32)
        ).astype(jnp.bfloat16)
        whole_reduced = group_gather(reduced, height)
        result = jnp.dot(inverse_block, whole_reduced, preferred_element_type=jnp.float32).astype(
            jnp.bfloat16
        )
        solved.append(result)
        top = result
    samples = [None] * levels
    correction = None
    for height in range(levels, 0, -1):
        span = 2**height * sections * row_count
        offset = (2**height - 2) * sections * row_count
        panel = sep_panel[:, offset : offset + span]
        inverse_block = sep_inv[:, offset : offset + span]
        summed = solved[height - 1].astype(jnp.float32) + sep_noise[height - 1].astype(jnp.float32)
        if correction is not None:
            summed = summed - correction
        vector = summed.astype(jnp.bfloat16)
        backed = group_reduce(transposed_dot(inverse_block, vector), height).astype(
            jnp.bfloat16
        )
        samples[height - 1] = (
            sep_dev[height - 1][:, None].astype(jnp.float32) * backed.astype(jnp.float32)
        ).astype(jnp.bfloat16)
        correction = group_reduce(transposed_dot(panel, backed), height)
    leading = jnp.zeros((subtree_row_count - row_count, correction.shape[1]), jnp.float32)
    placed = jnp.concatenate([leading, correction], axis=0)
    subtree_summed = (
        subtree_forward_solution.astype(jnp.float32) + leaf_noise.astype(jnp.float32) - placed
    )
    subtree_weight = jnp.where(row_activity, subtree_summed, jnp.float32(0.0)).astype(jnp.bfloat16)
    subtree_solution = transposed_dot(leaf_inv, subtree_weight)
    sample_scales = leaf_dev[:, None].astype(jnp.float32)
    subtree_scaled_samples = jnp.where(
        row_activity, sample_scales * subtree_solution, jnp.float32(0.0)
    ).astype(jnp.bfloat16)
    return (subtree_scaled_samples, jnp.stack(samples))


def on_device(
    leaf_inv,
    subtree_blocks,
    subtree_shift_rhs,
    leaf_noise,
    leaf_dev,
    sep_inv,
    sep_panel,
    sep_rhs,
    sep_noise,
    sep_dev,
):
    subtree_rows = leaf_inv.shape[0]
    row_count = sep_inv.shape[0]
    levels, _, samples = sep_rhs.shape
    unit = 2 * row_count
    vmem = pl.BlockSpec(memory_space=pltpu.VMEM)
    smem = pl.BlockSpec(memory_space=pltpu.SMEM)

    def params(mib):
        return pltpu.CompilerParams(vmem_limit_bytes=mib * 2**20)

    top_columns = 2 * 2**levels * unit + 2 * samples
    low_columns = samples + sum(2 * 2**h * unit + 2 * samples for h in range(1, levels))
    hbm = pl.BlockSpec(memory_space=pltpu.HBM)

    def in_hbm(array):
        return pltpu.with_memory_space_constraint(array, pltpu.HBM)

    low, top = pl.pallas_call(
        functools.partial(pack_kernel, levels),
        out_shape=(
            jax.ShapeDtypeStruct((row_count, low_columns), jnp.bfloat16),
            jax.ShapeDtypeStruct((row_count, top_columns), jnp.bfloat16),
        ),
        in_specs=[smem] + [hbm] * 6,
        out_specs=(vmem, vmem),
        scratch_shapes=[
            pltpu.VMEM((row_count, subtree_rows), jnp.bfloat16),
            pltpu.VMEM(subtree_shift_rhs.shape, jnp.bfloat16),
            pltpu.VMEM(sep_panel.shape, jnp.bfloat16),
            pltpu.VMEM(sep_inv.shape, jnp.bfloat16),
            pltpu.VMEM(sep_rhs.shape, jnp.bfloat16),
            pltpu.VMEM(sep_noise.shape, jnp.bfloat16),
            pltpu.SemaphoreType.DMA((6,)),
        ],
        compiler_params=params(4),
        name="pack",
    )(subtree_blocks, *(in_hbm(x) for x in (leaf_inv, subtree_shift_rhs, sep_panel, sep_inv, sep_rhs, sep_noise)))

    def swap(block):
        return lax.ppermute(block, "sec", [(0, 1), (1, 0)])

    def join(arrays, *after, flops=0):
        rows = sum(array.shape[0] for array in arrays)
        return pl.pallas_call(
            lambda *refs: join_kernel(*refs[len(after) :]),
            out_shape=jax.ShapeDtypeStruct((rows, arrays[0].shape[1]), arrays[0].dtype),
            in_specs=[pl.BlockSpec(memory_space=pl.ANY)] * len(after) + [vmem] * len(arrays),
            out_specs=vmem,
            compiler_params=params(4),
            cost_estimate=pl.CostEstimate(flops=flops, bytes_accessed=0, transcendentals=0) if flops else None,
            name="join",
        )(*after, *arrays)

    quad = 2 ** (levels - 1)
    near = join([low] + [to_chips(low, (distance, distance)) for distance in range(1, quad)])
    passed = swap(near)
    quarter = []
    for turned, array in enumerate((near, passed)):
        for distance in range(quad):
            quarter.append((array, distance * row_count, (distance, distance), turned))

    top_other = swap(top)
    top_pair = join([top, top_other], flops=10**10)

    def listed(pieces):
        arrays, places = [], []
        for array, start, distances, turned in pieces:
            if not any(array is known for known in arrays):
                arrays.append(array)
            which = [array is known for known in arrays].index(True)
            places.append((which, start, distances, turned))
        return arrays, places

    base, edge, inner, scale, sep_scale = pl.pallas_call(
        functools.partial(leaf_kernel, row_count),
        out_shape=(
            jax.ShapeDtypeStruct((subtree_rows, samples), jnp.float32),
            jax.ShapeDtypeStruct((row_count, samples), jnp.float32),
            jax.ShapeDtypeStruct((subtree_rows, row_count), jnp.bfloat16),
            jax.ShapeDtypeStruct((subtree_rows, samples), jnp.float32),
            jax.ShapeDtypeStruct((levels, row_count, samples), jnp.float32),
        ),
        in_specs=[smem] + [vmem] * 5,
        out_specs=(vmem,) * 5,
        compiler_params=params(12),
        cost_estimate=pl.CostEstimate(flops=10**10, bytes_accessed=1, transcendentals=0),
        name="leaf",
    )(subtree_blocks, leaf_inv, subtree_shift_rhs, leaf_noise, leaf_dev[None, :], sep_dev)

    arrays, places = listed(quarter)
    low_whole, *solved = pl.pallas_call(
        functools.partial(low_kernel, levels, unit, places),
        out_shape=[jax.ShapeDtypeStruct((quad * unit, low_columns), jnp.bfloat16)]
        + [jax.ShapeDtypeStruct((quad * unit, samples), jnp.bfloat16)] * (levels - 1),
        in_specs=[vmem] * len(arrays) + [pl.BlockSpec(memory_space=pl.ANY)],
        out_specs=[vmem] * levels,
        compiler_params=params(8),
        name="low",
    )(*arrays, edge)
    partner = to_chips(solved[-1], (quad, quad))

    trips = [(join([top], top_pair), (2, 2)), (top_pair, (1, 3)), (top_pair, (4, 5)), (top_pair, (6, 7))]
    far = [(top, 0, (0, 0), 0), (top_other, 0, (0, 0), 1)]
    arrived = [to_chips(block, distances) for block, distances in trips]
    for chosen in ((2, 3), (0, 1)):
        here = join([arrived[index] for index in chosen], solved[-1])
        there = swap(here)
        row = 0
        for block, (first, second) in (trips[index] for index in chosen):
            for turned in range(block.shape[0] // row_count):
                far.append((here, row, (first, second), turned))
                far.append((there, row, (second, first), 1 - turned))
                row += row_count

    edge = join([edge], partner, flops=10**10)
    arrays, places = listed(far)
    span = 2**levels * unit
    return pl.pallas_call(
        functools.partial(top_kernel, levels, unit, places),
        out_shape=(
            jax.ShapeDtypeStruct((subtree_rows, samples), jnp.bfloat16),
            jax.ShapeDtypeStruct((levels, row_count, samples), jnp.bfloat16),
        ),
        in_specs=[vmem] * (7 + levels - 1 + len(arrays)),
        out_specs=(vmem, vmem),
        scratch_shapes=[
            pltpu.VMEM((span, top_columns), jnp.bfloat16),
            pltpu.VMEM((span, samples), jnp.bfloat16),
            pltpu.VMEM((span, samples), jnp.float32),
            pltpu.VMEM((unit * 2, samples), jnp.float32),
        ],
        compiler_params=params(16),
        name="top",
    )(low_whole, sep_scale, partner, base, edge, inner, scale, *solved, *arrays)


def solution(mesh):
    rows = P(AXES, None)
    in_specs = (
        rows,
        P("leaf", "sec"),
        rows,
        rows,
        P(AXES),
        rows,
        rows,
        P(None, AXES, None),
        P(None, AXES, None),
        P(None, AXES),
    )
    out_specs = (rows, P(None, AXES, None))

    def program(*arrays):
        levels = arrays[7].shape[0]
        paired = levels == 3 and mesh.shape["sec"] == 2 and mesh.shape["leaf"] % 2**levels == 0
        return on_device(*arrays) if paired else leafwise_on_device(*arrays)

    return jax.shard_map(program, mesh=mesh, in_specs=in_specs, out_specs=out_specs, check_vma=False)
```

```python
import functools

import jax
import jax.numpy as jnp
from jax import lax
from jax.experimental import pallas as pl
from jax.experimental.pallas import tpu as pltpu
from jax.sharding import PartitionSpec as P

BLOCK = 128
AXES = ("leaf", "sec")


def to_chips(block, distances):
    leaves, sections = lax.axis_size("leaf"), lax.axis_size("sec")
    route = []
    for leaf in range(leaves):
        for section, distance in enumerate(distances):
            route.append((leaf * sections + section, (leaf ^ distance) * sections + section))
    return lax.ppermute(block, AXES, route)


def column_of(row):
    count = row.shape[1]
    across = lax.broadcasted_iota(jnp.int32, (count, count), 1)
    down = lax.broadcasted_iota(jnp.int32, (count, count), 0)
    return jnp.sum(jnp.where(across == down, row, jnp.zeros_like(row)), axis=1, keepdims=True)


def live_rows(blocks_ref, shape, dimension):
    return lax.broadcasted_iota(jnp.int32, shape, dimension) >= shape[dimension] - blocks_ref[0, 0] * BLOCK


def pack_kernel(levels, blocks_ref, *refs):
    sources, (low_ref, top_ref), moved, arrived = refs[:6], refs[6:8], refs[8:14], refs[14]
    rows = sources[0].shape[0]
    row_count = moved[0].shape[0]
    parts = (sources[0].at[pl.ds(rows - row_count, row_count)],) + sources[1:]
    copies = [pltpu.make_async_copy(part, ref, arrived.at[n]) for n, (part, ref) in enumerate(zip(parts, moved))]
    for copy in copies:
        copy.start()
    edge_ref, shift_ref, panel_ref, inv_ref, rhs_ref, noise_ref = moved
    samples = shift_ref.shape[1]
    for copy in copies[2:]:
        copy.wait()
    unit = panel_ref.shape[1] // (2 ** (levels + 1) - 2)
    at, offset = samples, 0
    for height in range(1, levels + 1):
        span = 2**height * unit
        out = low_ref if height < levels else top_ref
        at = at if height < levels else 0
        out[:, at : at + span] = panel_ref[:, offset : offset + span]
        out[:, at + span : at + 2 * span] = inv_ref[:, offset : offset + span]
        out[:, at + 2 * span : at + 2 * span + samples] = rhs_ref[height - 1]
        out[:, at + 2 * span + samples : at + 2 * span + 2 * samples] = noise_ref[height - 1]
        at += 2 * span + 2 * samples
        offset += span
    for copy in copies[:2]:
        copy.wait()
    inverse = edge_ref[...]
    inverse = jnp.where(live_rows(blocks_ref, inverse.shape, 1), inverse, jnp.zeros_like(inverse))
    boundary = jnp.dot(inverse, shift_ref[...], preferred_element_type=jnp.float32)
    low_ref[:, :samples] = boundary.astype(jnp.bfloat16)


def join_kernel(*refs):
    joined_ref, row = refs[-1], 0
    for ref in refs[:-1]:
        joined_ref[row : row + ref.shape[0], :] = ref[...]
        row += ref.shape[0]


def place(pieces, refs, whole_ref, row_count, leaves):
    leaf, section = lax.axis_index("leaf"), lax.axis_index("sec")
    for which, start, distances, turned in pieces:
        if isinstance(turned, int):
            owner = section ^ turned
            distance = jnp.where(section == 0, distances[0], distances[1])
        else:
            owner, distance = turned[0], distances[0]
        at = (((leaf ^ distance) & (leaves - 1)) * 2 + owner) * row_count
        ref = refs[which]
        whole_ref[pl.ds(pl.multiple_of(at, row_count), row_count), :] = ref[start : start + row_count, :]


def solve_forward(whole, rows, at, span, samples, children):
    panel = whole[rows, at : at + span]
    inverse = whole[rows, at + span : at + 2 * span]
    rhs = whole[rows, at + 2 * span : at + 2 * span + samples]
    reduced = rhs.astype(jnp.float32) - jnp.dot(panel, children, preferred_element_type=jnp.float32)
    reduced = reduced.astype(jnp.bfloat16)
    return jnp.dot(inverse, reduced, preferred_element_type=jnp.float32).astype(jnp.bfloat16)


def low_kernel(levels, unit, pieces, *refs):
    piece_refs, (whole_ref, *solved_refs) = refs[: -levels - 1], refs[-levels:]
    row_count = unit // 2
    place(pieces, piece_refs, whole_ref, row_count, 2 ** (levels - 1))
    samples = solved_refs[0].shape[1]
    total = whole_ref.shape[0]
    below_ref, at = whole_ref, samples
    for height in range(1, levels):
        span = 2**height * unit
        for group in range(total // span):
            rows = slice(group * span, (group + 1) * span)
            children = below_ref[rows, 0:samples]
            solved_refs[height - 1][rows, :] = solve_forward(whole_ref, rows, at, span, samples, children)
        below_ref = solved_refs[height - 1]
        at += 2 * span + 2 * samples


def leaf_kernel(
    row_count,
    blocks_ref,
    leaf_ref,
    shift_ref,
    noise_ref,
    dev_ref,
    sep_dev_ref,
    base_ref,
    edge_ref,
    inner_ref,
    scale_ref,
    sep_scale_ref,
):
    rows, samples = shift_ref.shape
    live = live_rows(blocks_ref, (rows, samples), 0)
    shift = shift_ref[...]
    shift = jnp.where(live, shift, jnp.zeros_like(shift))
    zero = jnp.float32(0.0)
    forward = jnp.dot(leaf_ref[...], shift, preferred_element_type=jnp.float32)
    forward = jnp.where(live, forward, zero).astype(jnp.bfloat16)
    summed = forward.astype(jnp.float32) + noise_ref[...].astype(jnp.float32)
    inner = rows - row_count
    edge_ref[...] = summed[inner:, :]
    within = lax.broadcasted_iota(jnp.int32, (rows, samples), 0) < inner
    weight = jnp.where(live & within, summed, zero)
    product = jnp.dot(weight.T.astype(jnp.bfloat16), leaf_ref[...], preferred_element_type=jnp.float32)
    base_ref[...] = product.T
    inner_ref[...] = leaf_ref[inner:, :].astype(jnp.float32).T.astype(jnp.bfloat16)
    for block in range(rows // BLOCK):
        part = slice(block * BLOCK, (block + 1) * BLOCK)
        column = column_of(dev_ref[:, part].astype(jnp.float32))
        scale_ref[part, :] = jnp.where(live[part, :], jnp.broadcast_to(column, (BLOCK, samples)), zero)
    for height in range(sep_scale_ref.shape[0]):
        column = column_of(sep_dev_ref[height : height + 1, :].astype(jnp.float32))
        sep_scale_ref[height] = jnp.broadcast_to(column, (row_count, samples))


def top_kernel(levels, unit, pieces, *refs):
    low_ref, sep_scale_ref, partner_ref, base_ref, edge_ref, inner_ref, scale_ref = refs[:7]
    solved_refs = refs[7 : 7 + levels - 1]
    out_ref, sample_ref, whole_ref, child_ref, x_ref, sum_ref = refs[-6:]
    piece_refs = refs[7 + levels - 1 : -6]
    samples = partner_ref.shape[1]
    row_count = unit // 2
    leaf, section = lax.axis_index("leaf"), lax.axis_index("sec")
    place(pieces, piece_refs, whole_ref, row_count, 2**levels)
    half = partner_ref.shape[0]
    upper = leaf >> (levels - 1) & 1
    child_ref[pl.ds(pl.multiple_of(upper * half, half), half), :] = solved_refs[-1][...]
    child_ref[pl.ds(pl.multiple_of((1 - upper) * half, half), half), :] = partner_ref[...]
    top_span = 2**levels * unit
    own = solve_forward(whole_ref, slice(0, top_span), 0, top_span, samples, child_ref[...])
    correction = None
    low_at = low_ref.shape[1]
    for height in range(levels, 0, -1):
        span = 2**height * unit
        if height == levels:
            source, at, rows = whole_ref, 0, slice(0, span)
        else:
            low_at -= 2 * span + 2 * samples
            first = ((leaf & (2 ** (levels - 1) - 1)) >> height) * span
            source, at, rows = low_ref, low_at, pl.ds(pl.multiple_of(first, span), span)
            own = solved_refs[height - 1][rows, :]
        noise = source[rows, at + 2 * span + samples : at + 2 * span + 2 * samples]
        summed = (own.astype(jnp.float32) + noise.astype(jnp.float32)).T
        if correction is not None:
            summed = summed - correction
        x = jnp.dot(
            summed.astype(jnp.bfloat16), source[rows, at + span : at + 2 * span], preferred_element_type=jnp.float32
        ).astype(jnp.bfloat16)
        pushed = jnp.dot(x, source[rows, at : at + span], preferred_element_type=jnp.float32)
        x_ref[0:span, :] = x.astype(jnp.float32).T
        mine = pl.ds(pl.multiple_of(((leaf & (2**height - 1)) * 2 + section) * row_count, row_count), row_count)
        sample_ref[height - 1] = (sep_scale_ref[height - 1] * x_ref[mine, :]).astype(jnp.bfloat16)
        if height > 1:
            upper = leaf >> (height - 1) & 1
            correction = jnp.where(upper == 1, pushed[:, span // 2 :], pushed[:, : span // 2])
        else:
            sum_ref[...] = pushed.T
            correction = sum_ref[mine, :]
    weight = (edge_ref[...] - correction).astype(jnp.bfloat16)
    back = base_ref[...] + jnp.dot(inner_ref[...], weight, preferred_element_type=jnp.float32)
    out_ref[...] = (scale_ref[...] * back).astype(jnp.bfloat16)


def transposed_dot(matrix, vector):
    return lax.dot_general(matrix, vector, (((0,), (0,)), ((), ())), preferred_element_type=jnp.float32)


def from_partner(block, axis, apart):
    count = lax.axis_size(axis)
    route = []
    for low in range(count):
        high = low | 1 << apart
        if high != low and high < count:
            route += [(low, high), (high, low)]
    return lax.ppermute(block, axis, route)


def pair_gather(block, height):
    leaf_place = lax.axis_index("leaf")
    for bit_index in range(height):
        partner = from_partner(block, "leaf", bit_index)
        upper_half = leaf_place >> bit_index & 1 == 1
        block = jnp.where(
            upper_half, jnp.concatenate([partner, block], 0), jnp.concatenate([block, partner], 0)
        )
    return block


def group_gather(piece, height):
    block = lax.all_gather(piece, "sec", axis=0, tiled=True)
    return pair_gather(block, height)


def halve_pairs(partial_sum, height):
    leaf_place = lax.axis_index("leaf")
    for bit_index in reversed(range(height)):
        half_rows = partial_sum.shape[0] // 2
        lower_rows = partial_sum[:half_rows]
        upper_rows = partial_sum[half_rows:]
        upper_half = leaf_place >> bit_index & 1 == 1
        kept = jnp.where(upper_half, upper_rows, lower_rows)
        outgoing = jnp.where(upper_half, lower_rows, upper_rows)
        partial_sum = kept + from_partner(outgoing, "leaf", bit_index)
    return partial_sum


def group_reduce(partial_sum, height):
    reduced = halve_pairs(partial_sum, height)
    return lax.psum_scatter(reduced, "sec", scatter_dimension=0, tiled=True)


def leafwise_on_device(
    leaf_inv,
    subtree_blocks,
    subtree_shift_rhs,
    leaf_noise,
    leaf_dev,
    sep_inv,
    sep_panel,
    sep_rhs,
    sep_noise,
    sep_dev,
):
    subtree_row_count = leaf_inv.shape[0]
    row_count = sep_inv.shape[0]
    levels = sep_rhs.shape[0]
    sections = lax.axis_size("sec")
    active_rows = subtree_blocks[0, 0] * BLOCK
    row_positions = jnp.arange(subtree_row_count, dtype=jnp.int32)
    row_activity = (row_positions >= subtree_row_count - active_rows)[:, None]
    subtree_shifted = jnp.where(
        row_activity, subtree_shift_rhs, jnp.zeros((), subtree_shift_rhs.dtype)
    )
    forward_subtree = jnp.dot(leaf_inv, subtree_shifted, preferred_element_type=jnp.float32)
    subtree_forward_solution = jnp.where(row_activity, forward_subtree, jnp.float32(0.0)).astype(
        jnp.bfloat16
    )
    top = subtree_forward_solution[subtree_row_count - row_count :]
    solved = []
    for height in range(1, levels + 1):
        span = 2**height * sections * row_count
        offset = (2**height - 2) * sections * row_count
        children = group_gather(top, height)
        panel = sep_panel[:, offset : offset + span]
        inverse_block = sep_inv[:, offset : offset + span]
        reduced = (
            sep_rhs[height - 1].astype(jnp.float32)
            - jnp.dot(panel, children, preferred_element_type=jnp.float32)
        ).astype(jnp.bfloat16)
        whole_reduced = group_gather(reduced, height)
        result = jnp.dot(inverse_block, whole_reduced, preferred_element_type=jnp.float32).astype(
            jnp.bfloat16
        )
        solved.append(result)
        top = result
    samples = [None] * levels
    correction = None
    for height in range(levels, 0, -1):
        span = 2**height * sections * row_count
        offset = (2**height - 2) * sections * row_count
        panel = sep_panel[:, offset : offset + span]
        inverse_block = sep_inv[:, offset : offset + span]
        summed = solved[height - 1].astype(jnp.float32) + sep_noise[height - 1].astype(jnp.float32)
        if correction is not None:
            summed = summed - correction
        vector = summed.astype(jnp.bfloat16)
        backed = group_reduce(transposed_dot(inverse_block, vector), height).astype(
            jnp.bfloat16
        )
        samples[height - 1] = (
            sep_dev[height - 1][:, None].astype(jnp.float32) * backed.astype(jnp.float32)
        ).astype(jnp.bfloat16)
        correction = group_reduce(transposed_dot(panel, backed), height)
    leading = jnp.zeros((subtree_row_count - row_count, correction.shape[1]), jnp.float32)
    placed = jnp.concatenate([leading, correction], axis=0)
    subtree_summed = (
        subtree_forward_solution.astype(jnp.float32) + leaf_noise.astype(jnp.float32) - placed
    )
    subtree_weight = jnp.where(row_activity, subtree_summed, jnp.float32(0.0)).astype(jnp.bfloat16)
    subtree_solution = transposed_dot(leaf_inv, subtree_weight)
    sample_scales = leaf_dev[:, None].astype(jnp.float32)
    subtree_scaled_samples = jnp.where(
        row_activity, sample_scales * subtree_solution, jnp.float32(0.0)
    ).astype(jnp.bfloat16)
    return (subtree_scaled_samples, jnp.stack(samples))


def on_device(
    leaf_inv,
    subtree_blocks,
    subtree_shift_rhs,
    leaf_noise,
    leaf_dev,
    sep_inv,
    sep_panel,
    sep_rhs,
    sep_noise,
    sep_dev,
):
    subtree_rows = leaf_inv.shape[0]
    row_count = sep_inv.shape[0]
    levels, _, samples = sep_rhs.shape
    unit = 2 * row_count
    vmem = pl.BlockSpec(memory_space=pltpu.VMEM)
    smem = pl.BlockSpec(memory_space=pltpu.SMEM)

    def params(mib):
        return pltpu.CompilerParams(vmem_limit_bytes=mib * 2**20)

    top_columns = 2 * 2**levels * unit + 2 * samples
    low_columns = samples + sum(2 * 2**h * unit + 2 * samples for h in range(1, levels))
    hbm = pl.BlockSpec(memory_space=pltpu.HBM)

    def in_hbm(array):
        return pltpu.with_memory_space_constraint(array, pltpu.HBM)

    low, top = pl.pallas_call(
        functools.partial(pack_kernel, levels),
        out_shape=(
            jax.ShapeDtypeStruct((row_count, low_columns), jnp.bfloat16),
            jax.ShapeDtypeStruct((row_count, top_columns), jnp.bfloat16),
        ),
        in_specs=[smem] + [hbm] * 6,
        out_specs=(vmem, vmem),
        scratch_shapes=[
            pltpu.VMEM((row_count, subtree_rows), jnp.bfloat16),
            pltpu.VMEM(subtree_shift_rhs.shape, jnp.bfloat16),
            pltpu.VMEM(sep_panel.shape, jnp.bfloat16),
            pltpu.VMEM(sep_inv.shape, jnp.bfloat16),
            pltpu.VMEM(sep_rhs.shape, jnp.bfloat16),
            pltpu.VMEM(sep_noise.shape, jnp.bfloat16),
            pltpu.SemaphoreType.DMA((6,)),
        ],
        compiler_params=params(4),
        name="pack",
    )(subtree_blocks, *(in_hbm(x) for x in (leaf_inv, subtree_shift_rhs, sep_panel, sep_inv, sep_rhs, sep_noise)))

    def swap(block):
        return lax.ppermute(block, "sec", [(0, 1), (1, 0)])

    def join(arrays, *after, flops=0):
        rows = sum(array.shape[0] for array in arrays)
        return pl.pallas_call(
            lambda *refs: join_kernel(*refs[len(after) :]),
            out_shape=jax.ShapeDtypeStruct((rows, arrays[0].shape[1]), arrays[0].dtype),
            in_specs=[pl.BlockSpec(memory_space=pl.ANY)] * len(after) + [vmem] * len(arrays),
            out_specs=vmem,
            compiler_params=params(4),
            cost_estimate=pl.CostEstimate(flops=flops, bytes_accessed=0, transcendentals=0) if flops else None,
            name="join",
        )(*after, *arrays)

    quad = 2 ** (levels - 1)
    near = join([low] + [to_chips(low, (distance, distance)) for distance in range(1, quad)])
    passed = swap(near)
    quarter = []
    for turned, array in enumerate((near, passed)):
        for distance in range(quad):
            quarter.append((array, distance * row_count, (distance, distance), turned))

    top_other = swap(top)
    top_pair = join([top, top_other], flops=10**10)

    def listed(pieces):
        arrays, places = [], []
        for array, start, distances, turned in pieces:
            if not any(array is known for known in arrays):
                arrays.append(array)
            which = [array is known for known in arrays].index(True)
            places.append((which, start, distances, turned))
        return arrays, places

    base, edge, inner, scale, sep_scale = pl.pallas_call(
        functools.partial(leaf_kernel, row_count),
        out_shape=(
            jax.ShapeDtypeStruct((subtree_rows, samples), jnp.float32),
            jax.ShapeDtypeStruct((row_count, samples), jnp.float32),
            jax.ShapeDtypeStruct((subtree_rows, row_count), jnp.bfloat16),
            jax.ShapeDtypeStruct((subtree_rows, samples), jnp.float32),
            jax.ShapeDtypeStruct((levels, row_count, samples), jnp.float32),
        ),
        in_specs=[smem] + [vmem] * 5,
        out_specs=(vmem,) * 5,
        compiler_params=params(12),
        cost_estimate=pl.CostEstimate(flops=10**10, bytes_accessed=1, transcendentals=0),
        name="leaf",
    )(subtree_blocks, leaf_inv, subtree_shift_rhs, leaf_noise, leaf_dev[None, :], sep_dev)

    arrays, places = listed(quarter)
    low_whole, *solved = pl.pallas_call(
        functools.partial(low_kernel, levels, unit, places),
        out_shape=[jax.ShapeDtypeStruct((quad * unit, low_columns), jnp.bfloat16)]
        + [jax.ShapeDtypeStruct((quad * unit, samples), jnp.bfloat16)] * (levels - 1),
        in_specs=[vmem] * len(arrays) + [pl.BlockSpec(memory_space=pl.ANY)],
        out_specs=[vmem] * levels,
        compiler_params=params(8),
        name="low",
    )(*arrays, edge)
    partner = to_chips(solved[-1], (quad, quad))

    trips = [(join([top], top_pair), (1, 1)), (top_pair, (3, 2)), (top_pair, (4, 5)), (top_pair, (6, 7))]
    far = [(top, 0, (0, 0), 0), (top_other, 0, (0, 0), 1)]
    arrived = [to_chips(block, distances) for block, distances in trips]
    for chosen in ((2, 3), (0, 1)):
        here = join([arrived[index] for index in chosen], solved[-1])
        there = swap(here)
        row = 0
        for block, (first, second) in (trips[index] for index in chosen):
            for turned in range(block.shape[0] // row_count):
                far.append((here, row, (first, second), turned))
                far.append((there, row, (second, first), 1 - turned))
                row += row_count

    edge = join([edge], partner, flops=10**10)
    arrays, places = listed(far)
    span = 2**levels * unit
    return pl.pallas_call(
        functools.partial(top_kernel, levels, unit, places),
        out_shape=(
            jax.ShapeDtypeStruct((subtree_rows, samples), jnp.bfloat16),
            jax.ShapeDtypeStruct((levels, row_count, samples), jnp.bfloat16),
        ),
        in_specs=[vmem] * (7 + levels - 1 + len(arrays)),
        out_specs=(vmem, vmem),
        scratch_shapes=[
            pltpu.VMEM((span, top_columns), jnp.bfloat16),
            pltpu.VMEM((span, samples), jnp.bfloat16),
            pltpu.VMEM((span, samples), jnp.float32),
            pltpu.VMEM((unit * 2, samples), jnp.float32),
        ],
        compiler_params=params(16),
        name="top",
    )(low_whole, sep_scale, partner, base, edge, inner, scale, *solved, *arrays)


def solution(mesh):
    rows = P(AXES, None)
    in_specs = (
        rows,
        P("leaf", "sec"),
        rows,
        rows,
        P(AXES),
        rows,
        rows,
        P(None, AXES, None),
        P(None, AXES, None),
        P(None, AXES),
    )
    out_specs = (rows, P(None, AXES, None))

    def program(*arrays):
        levels = arrays[7].shape[0]
        paired = levels == 3 and mesh.shape["sec"] == 2 and mesh.shape["leaf"] % 2**levels == 0
        return on_device(*arrays) if paired else leafwise_on_device(*arrays)

    return jax.shard_map(program, mesh=mesh, in_specs=in_specs, out_specs=out_specs, check_vma=False)
```

```python
import functools

import jax
import jax.numpy as jnp
from jax import lax
from jax.experimental import pallas as pl
from jax.experimental.pallas import tpu as pltpu
from jax.sharding import PartitionSpec as P

BLOCK = 128
AXES = ("leaf", "sec")


def to_chips(block, distances):
    leaves, sections = lax.axis_size("leaf"), lax.axis_size("sec")
    route = []
    for leaf in range(leaves):
        for section, distance in enumerate(distances):
            route.append((leaf * sections + section, (leaf ^ distance) * sections + section))
    return lax.ppermute(block, AXES, route)


def column_of(row):
    count = row.shape[1]
    across = lax.broadcasted_iota(jnp.int32, (count, count), 1)
    down = lax.broadcasted_iota(jnp.int32, (count, count), 0)
    return jnp.sum(jnp.where(across == down, row, jnp.zeros_like(row)), axis=1, keepdims=True)


def live_rows(blocks_ref, shape, dimension):
    return lax.broadcasted_iota(jnp.int32, shape, dimension) >= shape[dimension] - blocks_ref[0, 0] * BLOCK


def pack_kernel(levels, blocks_ref, *refs):
    sources, (low_ref, top_ref), moved, arrived = refs[:6], refs[6:8], refs[8:14], refs[14]
    rows = sources[0].shape[0]
    row_count = moved[0].shape[0]
    parts = (sources[0].at[pl.ds(rows - row_count, row_count)],) + sources[1:]
    copies = [pltpu.make_async_copy(part, ref, arrived.at[n]) for n, (part, ref) in enumerate(zip(parts, moved))]
    for copy in copies:
        copy.start()
    edge_ref, shift_ref, panel_ref, inv_ref, rhs_ref, noise_ref = moved
    samples = shift_ref.shape[1]
    for copy in copies[2:]:
        copy.wait()
    unit = panel_ref.shape[1] // (2 ** (levels + 1) - 2)
    at, offset = samples, 0
    for height in range(1, levels + 1):
        span = 2**height * unit
        out = low_ref if height < levels else top_ref
        at = at if height < levels else 0
        out[:, at : at + span] = panel_ref[:, offset : offset + span]
        out[:, at + span : at + 2 * span] = inv_ref[:, offset : offset + span]
        out[:, at + 2 * span : at + 2 * span + samples] = rhs_ref[height - 1]
        out[:, at + 2 * span + samples : at + 2 * span + 2 * samples] = noise_ref[height - 1]
        at += 2 * span + 2 * samples
        offset += span
    for copy in copies[:2]:
        copy.wait()
    inverse = edge_ref[...]
    inverse = jnp.where(live_rows(blocks_ref, inverse.shape, 1), inverse, jnp.zeros_like(inverse))
    boundary = jnp.dot(inverse, shift_ref[...], preferred_element_type=jnp.float32)
    low_ref[:, :samples] = boundary.astype(jnp.bfloat16)


def join_kernel(*refs):
    joined_ref, row = refs[-1], 0
    for ref in refs[:-1]:
        joined_ref[row : row + ref.shape[0], :] = ref[...]
        row += ref.shape[0]


def place(pieces, refs, whole_ref, row_count, leaves):
    leaf, section = lax.axis_index("leaf"), lax.axis_index("sec")
    for which, start, distances, turned in pieces:
        if isinstance(turned, int):
            owner = section ^ turned
            distance = jnp.where(section == 0, distances[0], distances[1])
        else:
            owner, distance = turned[0], distances[0]
        at = (((leaf ^ distance) & (leaves - 1)) * 2 + owner) * row_count
        ref = refs[which]
        whole_ref[pl.ds(pl.multiple_of(at, row_count), row_count), :] = ref[start : start + row_count, :]


def solve_forward(whole, rows, at, span, samples, children):
    panel = whole[rows, at : at + span]
    inverse = whole[rows, at + span : at + 2 * span]
    rhs = whole[rows, at + 2 * span : at + 2 * span + samples]
    reduced = rhs.astype(jnp.float32) - jnp.dot(panel, children, preferred_element_type=jnp.float32)
    reduced = reduced.astype(jnp.bfloat16)
    return jnp.dot(inverse, reduced, preferred_element_type=jnp.float32).astype(jnp.bfloat16)


def low_kernel(levels, unit, pieces, *refs):
    piece_refs, (whole_ref, *solved_refs) = refs[: -levels - 1], refs[-levels:]
    row_count = unit // 2
    place(pieces, piece_refs, whole_ref, row_count, 2 ** (levels - 1))
    samples = solved_refs[0].shape[1]
    total = whole_ref.shape[0]
    below_ref, at = whole_ref, samples
    for height in range(1, levels):
        span = 2**height * unit
        for group in range(total // span):
            rows = slice(group * span, (group + 1) * span)
            children = below_ref[rows, 0:samples]
            solved_refs[height - 1][rows, :] = solve_forward(whole_ref, rows, at, span, samples, children)
        below_ref = solved_refs[height - 1]
        at += 2 * span + 2 * samples


def leaf_kernel(
    row_count,
    blocks_ref,
    leaf_ref,
    shift_ref,
    noise_ref,
    dev_ref,
    sep_dev_ref,
    base_ref,
    edge_ref,
    inner_ref,
    scale_ref,
    sep_scale_ref,
):
    rows, samples = shift_ref.shape
    live = live_rows(blocks_ref, (rows, samples), 0)
    shift = shift_ref[...]
    shift = jnp.where(live, shift, jnp.zeros_like(shift))
    zero = jnp.float32(0.0)
    forward = jnp.dot(leaf_ref[...], shift, preferred_element_type=jnp.float32)
    forward = jnp.where(live, forward, zero).astype(jnp.bfloat16)
    summed = forward.astype(jnp.float32) + noise_ref[...].astype(jnp.float32)
    inner = rows - row_count
    edge_ref[...] = summed[inner:, :]
    within = lax.broadcasted_iota(jnp.int32, (rows, samples), 0) < inner
    weight = jnp.where(live & within, summed, zero)
    product = jnp.dot(weight.T.astype(jnp.bfloat16), leaf_ref[...], preferred_element_type=jnp.float32)
    base_ref[...] = product.T
    inner_ref[...] = leaf_ref[inner:, :].astype(jnp.float32).T.astype(jnp.bfloat16)
    for block in range(rows // BLOCK):
        part = slice(block * BLOCK, (block + 1) * BLOCK)
        column = column_of(dev_ref[:, part].astype(jnp.float32))
        scale_ref[part, :] = jnp.where(live[part, :], jnp.broadcast_to(column, (BLOCK, samples)), zero)
    for height in range(sep_scale_ref.shape[0]):
        column = column_of(sep_dev_ref[height : height + 1, :].astype(jnp.float32))
        sep_scale_ref[height] = jnp.broadcast_to(column, (row_count, samples))


def top_kernel(levels, unit, pieces, *refs):
    low_ref, sep_scale_ref, partner_ref, base_ref, edge_ref, inner_ref, scale_ref = refs[:7]
    solved_refs = refs[7 : 7 + levels - 1]
    out_ref, sample_ref, whole_ref, child_ref, x_ref, sum_ref = refs[-6:]
    piece_refs = refs[7 + levels - 1 : -6]
    samples = partner_ref.shape[1]
    row_count = unit // 2
    leaf, section = lax.axis_index("leaf"), lax.axis_index("sec")
    place(pieces, piece_refs, whole_ref, row_count, 2**levels)
    half = partner_ref.shape[0]
    upper = leaf >> (levels - 1) & 1
    child_ref[pl.ds(pl.multiple_of(upper * half, half), half), :] = solved_refs[-1][...]
    child_ref[pl.ds(pl.multiple_of((1 - upper) * half, half), half), :] = partner_ref[...]
    top_span = 2**levels * unit
    across = (((1,), (1,)), ((), ()))
    children = child_ref[...].astype(jnp.float32).T.astype(jnp.bfloat16)
    rhs = whole_ref[:, 2 * top_span : 2 * top_span + samples].astype(jnp.float32).T
    reduced = rhs - lax.dot_general(
        children, whole_ref[:, 0:top_span], across, preferred_element_type=jnp.float32
    )
    own = lax.dot_general(
        reduced.astype(jnp.bfloat16),
        whole_ref[:, top_span : 2 * top_span],
        across,
        preferred_element_type=jnp.float32,
    ).astype(jnp.bfloat16)
    correction = None
    low_at = low_ref.shape[1]
    for height in range(levels, 0, -1):
        span = 2**height * unit
        if height == levels:
            source, at, rows = whole_ref, 0, slice(0, span)
        else:
            low_at -= 2 * span + 2 * samples
            first = ((leaf & (2 ** (levels - 1) - 1)) >> height) * span
            source, at, rows = low_ref, low_at, pl.ds(pl.multiple_of(first, span), span)
            own = solved_refs[height - 1][rows, :]
        noise = source[rows, at + 2 * span + samples : at + 2 * span + 2 * samples]
        if height == levels:
            summed = own.astype(jnp.float32) + noise.astype(jnp.float32).T
        else:
            summed = (own.astype(jnp.float32) + noise.astype(jnp.float32)).T
        if correction is not None:
            summed = summed - correction
        x = jnp.dot(
            summed.astype(jnp.bfloat16), source[rows, at + span : at + 2 * span], preferred_element_type=jnp.float32
        ).astype(jnp.bfloat16)
        pushed = jnp.dot(x, source[rows, at : at + span], preferred_element_type=jnp.float32)
        x_ref[0:span, :] = x.astype(jnp.float32).T
        mine = pl.ds(pl.multiple_of(((leaf & (2**height - 1)) * 2 + section) * row_count, row_count), row_count)
        sample_ref[height - 1] = (sep_scale_ref[height - 1] * x_ref[mine, :]).astype(jnp.bfloat16)
        if height > 1:
            upper = leaf >> (height - 1) & 1
            correction = jnp.where(upper == 1, pushed[:, span // 2 :], pushed[:, : span // 2])
        else:
            sum_ref[...] = pushed.T
            correction = sum_ref[mine, :]
    weight = (edge_ref[...] - correction).astype(jnp.bfloat16)
    back = base_ref[...] + jnp.dot(inner_ref[...], weight, preferred_element_type=jnp.float32)
    out_ref[...] = (scale_ref[...] * back).astype(jnp.bfloat16)


def transposed_dot(matrix, vector):
    return lax.dot_general(matrix, vector, (((0,), (0,)), ((), ())), preferred_element_type=jnp.float32)


def from_partner(block, axis, apart):
    count = lax.axis_size(axis)
    route = []
    for low in range(count):
        high = low | 1 << apart
        if high != low and high < count:
            route += [(low, high), (high, low)]
    return lax.ppermute(block, axis, route)


def pair_gather(block, height):
    leaf_place = lax.axis_index("leaf")
    for bit_index in range(height):
        partner = from_partner(block, "leaf", bit_index)
        upper_half = leaf_place >> bit_index & 1 == 1
        block = jnp.where(
            upper_half, jnp.concatenate([partner, block], 0), jnp.concatenate([block, partner], 0)
        )
    return block


def group_gather(piece, height):
    block = lax.all_gather(piece, "sec", axis=0, tiled=True)
    return pair_gather(block, height)


def halve_pairs(partial_sum, height):
    leaf_place = lax.axis_index("leaf")
    for bit_index in reversed(range(height)):
        half_rows = partial_sum.shape[0] // 2
        lower_rows = partial_sum[:half_rows]
        upper_rows = partial_sum[half_rows:]
        upper_half = leaf_place >> bit_index & 1 == 1
        kept = jnp.where(upper_half, upper_rows, lower_rows)
        outgoing = jnp.where(upper_half, lower_rows, upper_rows)
        partial_sum = kept + from_partner(outgoing, "leaf", bit_index)
    return partial_sum


def group_reduce(partial_sum, height):
    reduced = halve_pairs(partial_sum, height)
    return lax.psum_scatter(reduced, "sec", scatter_dimension=0, tiled=True)


def leafwise_on_device(
    leaf_inv,
    subtree_blocks,
    subtree_shift_rhs,
    leaf_noise,
    leaf_dev,
    sep_inv,
    sep_panel,
    sep_rhs,
    sep_noise,
    sep_dev,
):
    subtree_row_count = leaf_inv.shape[0]
    row_count = sep_inv.shape[0]
    levels = sep_rhs.shape[0]
    sections = lax.axis_size("sec")
    active_rows = subtree_blocks[0, 0] * BLOCK
    row_positions = jnp.arange(subtree_row_count, dtype=jnp.int32)
    row_activity = (row_positions >= subtree_row_count - active_rows)[:, None]
    subtree_shifted = jnp.where(
        row_activity, subtree_shift_rhs, jnp.zeros((), subtree_shift_rhs.dtype)
    )
    forward_subtree = jnp.dot(leaf_inv, subtree_shifted, preferred_element_type=jnp.float32)
    subtree_forward_solution = jnp.where(row_activity, forward_subtree, jnp.float32(0.0)).astype(
        jnp.bfloat16
    )
    top = subtree_forward_solution[subtree_row_count - row_count :]
    solved = []
    for height in range(1, levels + 1):
        span = 2**height * sections * row_count
        offset = (2**height - 2) * sections * row_count
        children = group_gather(top, height)
        panel = sep_panel[:, offset : offset + span]
        inverse_block = sep_inv[:, offset : offset + span]
        reduced = (
            sep_rhs[height - 1].astype(jnp.float32)
            - jnp.dot(panel, children, preferred_element_type=jnp.float32)
        ).astype(jnp.bfloat16)
        whole_reduced = group_gather(reduced, height)
        result = jnp.dot(inverse_block, whole_reduced, preferred_element_type=jnp.float32).astype(
            jnp.bfloat16
        )
        solved.append(result)
        top = result
    samples = [None] * levels
    correction = None
    for height in range(levels, 0, -1):
        span = 2**height * sections * row_count
        offset = (2**height - 2) * sections * row_count
        panel = sep_panel[:, offset : offset + span]
        inverse_block = sep_inv[:, offset : offset + span]
        summed = solved[height - 1].astype(jnp.float32) + sep_noise[height - 1].astype(jnp.float32)
        if correction is not None:
            summed = summed - correction
        vector = summed.astype(jnp.bfloat16)
        backed = group_reduce(transposed_dot(inverse_block, vector), height).astype(
            jnp.bfloat16
        )
        samples[height - 1] = (
            sep_dev[height - 1][:, None].astype(jnp.float32) * backed.astype(jnp.float32)
        ).astype(jnp.bfloat16)
        correction = group_reduce(transposed_dot(panel, backed), height)
    leading = jnp.zeros((subtree_row_count - row_count, correction.shape[1]), jnp.float32)
    placed = jnp.concatenate([leading, correction], axis=0)
    subtree_summed = (
        subtree_forward_solution.astype(jnp.float32) + leaf_noise.astype(jnp.float32) - placed
    )
    subtree_weight = jnp.where(row_activity, subtree_summed, jnp.float32(0.0)).astype(jnp.bfloat16)
    subtree_solution = transposed_dot(leaf_inv, subtree_weight)
    sample_scales = leaf_dev[:, None].astype(jnp.float32)
    subtree_scaled_samples = jnp.where(
        row_activity, sample_scales * subtree_solution, jnp.float32(0.0)
    ).astype(jnp.bfloat16)
    return (subtree_scaled_samples, jnp.stack(samples))


def on_device(
    leaf_inv,
    subtree_blocks,
    subtree_shift_rhs,
    leaf_noise,
    leaf_dev,
    sep_inv,
    sep_panel,
    sep_rhs,
    sep_noise,
    sep_dev,
):
    subtree_rows = leaf_inv.shape[0]
    row_count = sep_inv.shape[0]
    levels, _, samples = sep_rhs.shape
    unit = 2 * row_count
    vmem = pl.BlockSpec(memory_space=pltpu.VMEM)
    smem = pl.BlockSpec(memory_space=pltpu.SMEM)

    def params(mib):
        return pltpu.CompilerParams(vmem_limit_bytes=mib * 2**20)

    top_columns = 2 * 2**levels * unit + 2 * samples
    low_columns = samples + sum(2 * 2**h * unit + 2 * samples for h in range(1, levels))
    hbm = pl.BlockSpec(memory_space=pltpu.HBM)

    def in_hbm(array):
        return pltpu.with_memory_space_constraint(array, pltpu.HBM)

    low, top = pl.pallas_call(
        functools.partial(pack_kernel, levels),
        out_shape=(
            jax.ShapeDtypeStruct((row_count, low_columns), jnp.bfloat16),
            jax.ShapeDtypeStruct((row_count, top_columns), jnp.bfloat16),
        ),
        in_specs=[smem] + [hbm] * 6,
        out_specs=(vmem, vmem),
        scratch_shapes=[
            pltpu.VMEM((row_count, subtree_rows), jnp.bfloat16),
            pltpu.VMEM(subtree_shift_rhs.shape, jnp.bfloat16),
            pltpu.VMEM(sep_panel.shape, jnp.bfloat16),
            pltpu.VMEM(sep_inv.shape, jnp.bfloat16),
            pltpu.VMEM(sep_rhs.shape, jnp.bfloat16),
            pltpu.VMEM(sep_noise.shape, jnp.bfloat16),
            pltpu.SemaphoreType.DMA((6,)),
        ],
        compiler_params=params(4),
        name="pack",
    )(subtree_blocks, *(in_hbm(x) for x in (leaf_inv, subtree_shift_rhs, sep_panel, sep_inv, sep_rhs, sep_noise)))

    def swap(block):
        return lax.ppermute(block, "sec", [(0, 1), (1, 0)])

    def join(arrays, *after, flops=0):
        rows = sum(array.shape[0] for array in arrays)
        return pl.pallas_call(
            lambda *refs: join_kernel(*refs[len(after) :]),
            out_shape=jax.ShapeDtypeStruct((rows, arrays[0].shape[1]), arrays[0].dtype),
            in_specs=[pl.BlockSpec(memory_space=pl.ANY)] * len(after) + [vmem] * len(arrays),
            out_specs=vmem,
            compiler_params=params(4),
            cost_estimate=pl.CostEstimate(flops=flops, bytes_accessed=0, transcendentals=0) if flops else None,
            name="join",
        )(*after, *arrays)

    quad = 2 ** (levels - 1)
    near = join([low] + [to_chips(low, (distance, distance)) for distance in range(1, quad)])
    passed = swap(near)
    quarter = []
    for turned, array in enumerate((near, passed)):
        for distance in range(quad):
            quarter.append((array, distance * row_count, (distance, distance), turned))

    top_other = swap(top)
    top_pair = join([top, top_other], flops=10**10)

    def listed(pieces):
        arrays, places = [], []
        for array, start, distances, turned in pieces:
            if not any(array is known for known in arrays):
                arrays.append(array)
            which = [array is known for known in arrays].index(True)
            places.append((which, start, distances, turned))
        return arrays, places

    base, edge, inner, scale, sep_scale = pl.pallas_call(
        functools.partial(leaf_kernel, row_count),
        out_shape=(
            jax.ShapeDtypeStruct((subtree_rows, samples), jnp.float32),
            jax.ShapeDtypeStruct((row_count, samples), jnp.float32),
            jax.ShapeDtypeStruct((subtree_rows, row_count), jnp.bfloat16),
            jax.ShapeDtypeStruct((subtree_rows, samples), jnp.float32),
            jax.ShapeDtypeStruct((levels, row_count, samples), jnp.float32),
        ),
        in_specs=[smem] + [vmem] * 5,
        out_specs=(vmem,) * 5,
        compiler_params=params(12),
        cost_estimate=pl.CostEstimate(flops=10**10, bytes_accessed=1, transcendentals=0),
        name="leaf",
    )(subtree_blocks, leaf_inv, subtree_shift_rhs, leaf_noise, leaf_dev[None, :], sep_dev)

    arrays, places = listed(quarter)
    low_whole, *solved = pl.pallas_call(
        functools.partial(low_kernel, levels, unit, places),
        out_shape=[jax.ShapeDtypeStruct((quad * unit, low_columns), jnp.bfloat16)]
        + [jax.ShapeDtypeStruct((quad * unit, samples), jnp.bfloat16)] * (levels - 1),
        in_specs=[vmem] * len(arrays) + [pl.BlockSpec(memory_space=pl.ANY)],
        out_specs=[vmem] * levels,
        compiler_params=params(8),
        name="low",
    )(*arrays, edge)
    partner = to_chips(solved[-1], (quad, quad))

    trips = [(join([top], top_pair), (1, 1)), (top_pair, (3, 2)), (top_pair, (4, 5)), (top_pair, (6, 7))]
    far = [(top, 0, (0, 0), 0), (top_other, 0, (0, 0), 1)]
    arrived = [to_chips(block, distances) for block, distances in trips]
    for chosen in ((2, 3, 0), (1,)):
        here = join([arrived[index] for index in chosen], solved[-1])
        there = swap(here)
        row = 0
        for block, (first, second) in (trips[index] for index in chosen):
            for turned in range(block.shape[0] // row_count):
                far.append((here, row, (first, second), turned))
                far.append((there, row, (second, first), 1 - turned))
                row += row_count

    edge = join([edge], partner, flops=10**10)
    arrays, places = listed(far)
    span = 2**levels * unit
    return pl.pallas_call(
        functools.partial(top_kernel, levels, unit, places),
        out_shape=(
            jax.ShapeDtypeStruct((subtree_rows, samples), jnp.bfloat16),
            jax.ShapeDtypeStruct((levels, row_count, samples), jnp.bfloat16),
        ),
        in_specs=[vmem] * (7 + levels - 1 + len(arrays)),
        out_specs=(vmem, vmem),
        scratch_shapes=[
            pltpu.VMEM((span, top_columns), jnp.bfloat16),
            pltpu.VMEM((span, samples), jnp.bfloat16),
            pltpu.VMEM((span, samples), jnp.float32),
            pltpu.VMEM((unit * 2, samples), jnp.float32),
        ],
        compiler_params=params(16),
        name="top",
    )(low_whole, sep_scale, partner, base, edge, inner, scale, *solved, *arrays)


def solution(mesh):
    rows = P(AXES, None)
    in_specs = (
        rows,
        P("leaf", "sec"),
        rows,
        rows,
        P(AXES),
        rows,
        rows,
        P(None, AXES, None),
        P(None, AXES, None),
        P(None, AXES),
    )
    out_specs = (rows, P(None, AXES, None))

    def program(*arrays):
        levels = arrays[7].shape[0]
        paired = levels == 3 and mesh.shape["sec"] == 2 and mesh.shape["leaf"] % 2**levels == 0
        return on_device(*arrays) if paired else leafwise_on_device(*arrays)

    return jax.shard_map(program, mesh=mesh, in_specs=in_specs, out_specs=out_specs, check_vma=False)
```

```python
import functools

import jax
import jax.numpy as jnp
from jax import lax
from jax.experimental import pallas as pl
from jax.experimental.pallas import tpu as pltpu
from jax.sharding import PartitionSpec as P

BLOCK = 128
AXES = ("leaf", "sec")


def to_chips(block, distances):
    leaves, sections = lax.axis_size("leaf"), lax.axis_size("sec")
    route = []
    for leaf in range(leaves):
        for section, distance in enumerate(distances):
            route.append((leaf * sections + section, (leaf ^ distance) * sections + section))
    return lax.ppermute(block, AXES, route)


def column_of(row):
    count = row.shape[1]
    across = lax.broadcasted_iota(jnp.int32, (count, count), 1)
    down = lax.broadcasted_iota(jnp.int32, (count, count), 0)
    return jnp.sum(jnp.where(across == down, row, jnp.zeros_like(row)), axis=1, keepdims=True)


def live_rows(blocks_ref, shape, dimension):
    return lax.broadcasted_iota(jnp.int32, shape, dimension) >= shape[dimension] - blocks_ref[0, 0] * BLOCK


def pack_kernel(levels, blocks_ref, *refs):
    sources, (low_ref, top_ref), moved, arrived = refs[:6], refs[6:8], refs[8:14], refs[14]
    rows = sources[0].shape[0]
    row_count = moved[0].shape[0]
    parts = (sources[0].at[pl.ds(rows - row_count, row_count)],) + sources[1:]
    copies = [pltpu.make_async_copy(part, ref, arrived.at[n]) for n, (part, ref) in enumerate(zip(parts, moved))]
    for copy in copies:
        copy.start()
    edge_ref, shift_ref, panel_ref, inv_ref, rhs_ref, noise_ref = moved
    samples = shift_ref.shape[1]
    for copy in copies[2:]:
        copy.wait()
    unit = panel_ref.shape[1] // (2 ** (levels + 1) - 2)
    at, offset = samples, 0
    for height in range(1, levels + 1):
        span = 2**height * unit
        out = low_ref if height < levels else top_ref
        at = at if height < levels else 0
        out[:, at : at + span] = panel_ref[:, offset : offset + span]
        out[:, at + span : at + 2 * span] = inv_ref[:, offset : offset + span]
        out[:, at + 2 * span : at + 2 * span + samples] = rhs_ref[height - 1]
        out[:, at + 2 * span + samples : at + 2 * span + 2 * samples] = noise_ref[height - 1]
        at += 2 * span + 2 * samples
        offset += span
    for copy in copies[:2]:
        copy.wait()
    inverse = edge_ref[...]
    inverse = jnp.where(live_rows(blocks_ref, inverse.shape, 1), inverse, jnp.zeros_like(inverse))
    boundary = jnp.dot(inverse, shift_ref[...], preferred_element_type=jnp.float32)
    low_ref[:, :samples] = boundary.astype(jnp.bfloat16)


def join_kernel(*refs):
    joined_ref, row = refs[-1], 0
    for ref in refs[:-1]:
        joined_ref[row : row + ref.shape[0], :] = ref[...]
        row += ref.shape[0]


def place(pieces, refs, whole_ref, row_count, leaves):
    leaf, section = lax.axis_index("leaf"), lax.axis_index("sec")
    for which, start, distances, turned in pieces:
        if isinstance(turned, int):
            owner = section ^ turned
            distance = jnp.where(section == 0, distances[0], distances[1])
        else:
            owner, distance = turned[0], distances[0]
        at = (((leaf ^ distance) & (leaves - 1)) * 2 + owner) * row_count
        ref = refs[which]
        whole_ref[pl.ds(pl.multiple_of(at, row_count), row_count), :] = ref[start : start + row_count, :]


def solve_forward(whole, rows, at, span, samples, children):
    panel = whole[rows, at : at + span]
    inverse = whole[rows, at + span : at + 2 * span]
    rhs = whole[rows, at + 2 * span : at + 2 * span + samples]
    reduced = rhs.astype(jnp.float32) - jnp.dot(panel, children, preferred_element_type=jnp.float32)
    reduced = reduced.astype(jnp.bfloat16)
    return jnp.dot(inverse, reduced, preferred_element_type=jnp.float32).astype(jnp.bfloat16)


def low_kernel(levels, unit, pieces, *refs):
    piece_refs, (whole_ref, *solved_refs) = refs[: -levels - 1], refs[-levels:]
    row_count = unit // 2
    place(pieces, piece_refs, whole_ref, row_count, 2 ** (levels - 1))
    samples = solved_refs[0].shape[1]
    total = whole_ref.shape[0]
    below_ref, at = whole_ref, samples
    for height in range(1, levels):
        span = 2**height * unit
        for group in range(total // span):
            rows = slice(group * span, (group + 1) * span)
            children = below_ref[rows, 0:samples]
            solved_refs[height - 1][rows, :] = solve_forward(whole_ref, rows, at, span, samples, children)
        below_ref = solved_refs[height - 1]
        at += 2 * span + 2 * samples


def leaf_kernel(
    row_count,
    blocks_ref,
    leaf_ref,
    shift_ref,
    noise_ref,
    dev_ref,
    sep_dev_ref,
    base_ref,
    edge_ref,
    inner_ref,
    scale_ref,
    sep_scale_ref,
):
    rows, samples = shift_ref.shape
    live = live_rows(blocks_ref, (rows, samples), 0)
    shift = shift_ref[...]
    shift = jnp.where(live, shift, jnp.zeros_like(shift))
    zero = jnp.float32(0.0)
    forward = jnp.dot(leaf_ref[...], shift, preferred_element_type=jnp.float32)
    forward = jnp.where(live, forward, zero).astype(jnp.bfloat16)
    summed = forward.astype(jnp.float32) + noise_ref[...].astype(jnp.float32)
    inner = rows - row_count
    edge_ref[...] = summed[inner:, :]
    within = lax.broadcasted_iota(jnp.int32, (rows, samples), 0) < inner
    weight = jnp.where(live & within, summed, zero)
    product = jnp.dot(weight.T.astype(jnp.bfloat16), leaf_ref[...], preferred_element_type=jnp.float32)
    base_ref[...] = product.T
    inner_ref[...] = leaf_ref[inner:, :].astype(jnp.float32).T.astype(jnp.bfloat16)
    deviations = dev_ref[...].astype(jnp.float32)
    sep_deviations = sep_dev_ref[...].astype(jnp.float32)
    for block in range(rows // BLOCK):
        part = slice(block * BLOCK, (block + 1) * BLOCK)
        column = column_of(deviations[:, part])
        scale_ref[part, :] = jnp.where(live[part, :], jnp.broadcast_to(column, (BLOCK, samples)), zero)
    for height in range(sep_scale_ref.shape[0]):
        column = column_of(sep_deviations[height : height + 1, :])
        sep_scale_ref[height] = jnp.broadcast_to(column, (row_count, samples))


def top_kernel(levels, unit, pieces, *refs):
    low_ref, sep_scale_ref, partner_ref, base_ref, edge_ref, inner_ref, scale_ref = refs[:7]
    solved_refs = refs[7 : 7 + levels - 1]
    out_ref, sample_ref, whole_ref, child_ref, x_ref, sum_ref = refs[-6:]
    piece_refs = refs[7 + levels - 1 : -6]
    samples = partner_ref.shape[1]
    row_count = unit // 2
    leaf, section = lax.axis_index("leaf"), lax.axis_index("sec")
    place(pieces, piece_refs, whole_ref, row_count, 2**levels)
    half = partner_ref.shape[0]
    upper = leaf >> (levels - 1) & 1
    child_ref[pl.ds(pl.multiple_of(upper * half, half), half), :] = solved_refs[-1][...]
    child_ref[pl.ds(pl.multiple_of((1 - upper) * half, half), half), :] = partner_ref[...]
    top_span = 2**levels * unit
    across = (((1,), (1,)), ((), ()))
    children = child_ref[...].astype(jnp.float32).T.astype(jnp.bfloat16)
    rhs = whole_ref[:, 2 * top_span : 2 * top_span + samples].astype(jnp.float32).T
    reduced = rhs - lax.dot_general(
        children, whole_ref[:, 0:top_span], across, preferred_element_type=jnp.float32
    )
    own = lax.dot_general(
        reduced.astype(jnp.bfloat16),
        whole_ref[:, top_span : 2 * top_span],
        across,
        preferred_element_type=jnp.float32,
    ).astype(jnp.bfloat16)
    correction = None
    low_at = low_ref.shape[1]
    for height in range(levels, 0, -1):
        span = 2**height * unit
        if height == levels:
            source, at, rows = whole_ref, 0, slice(0, span)
        else:
            low_at -= 2 * span + 2 * samples
            first = ((leaf & (2 ** (levels - 1) - 1)) >> height) * span
            source, at, rows = low_ref, low_at, pl.ds(pl.multiple_of(first, span), span)
            own = solved_refs[height - 1][rows, :]
        noise = source[rows, at + 2 * span + samples : at + 2 * span + 2 * samples]
        if height == levels:
            summed = own.astype(jnp.float32) + noise.astype(jnp.float32).T
        else:
            summed = (own.astype(jnp.float32) + noise.astype(jnp.float32)).T
        if correction is not None:
            summed = summed - correction
        x = jnp.dot(
            summed.astype(jnp.bfloat16), source[rows, at + span : at + 2 * span], preferred_element_type=jnp.float32
        ).astype(jnp.bfloat16)
        pushed = jnp.dot(x, source[rows, at : at + span], preferred_element_type=jnp.float32)
        x_ref[0:span, :] = x.astype(jnp.float32).T
        mine = pl.ds(pl.multiple_of(((leaf & (2**height - 1)) * 2 + section) * row_count, row_count), row_count)
        sample_ref[height - 1] = (sep_scale_ref[height - 1] * x_ref[mine, :]).astype(jnp.bfloat16)
        if height > 1:
            upper = leaf >> (height - 1) & 1
            correction = jnp.where(upper == 1, pushed[:, span // 2 :], pushed[:, : span // 2])
        else:
            sum_ref[...] = pushed.T
            correction = sum_ref[mine, :]
    weight = (edge_ref[...] - correction).astype(jnp.bfloat16)
    back = base_ref[...] + jnp.dot(inner_ref[...], weight, preferred_element_type=jnp.float32)
    out_ref[...] = (scale_ref[...] * back).astype(jnp.bfloat16)


def transposed_dot(matrix, vector):
    return lax.dot_general(matrix, vector, (((0,), (0,)), ((), ())), preferred_element_type=jnp.float32)


def from_partner(block, axis, apart):
    count = lax.axis_size(axis)
    route = []
    for low in range(count):
        high = low | 1 << apart
        if high != low and high < count:
            route += [(low, high), (high, low)]
    return lax.ppermute(block, axis, route)


def pair_gather(block, height):
    leaf_place = lax.axis_index("leaf")
    for bit_index in range(height):
        partner = from_partner(block, "leaf", bit_index)
        upper_half = leaf_place >> bit_index & 1 == 1
        block = jnp.where(
            upper_half, jnp.concatenate([partner, block], 0), jnp.concatenate([block, partner], 0)
        )
    return block


def group_gather(piece, height):
    block = lax.all_gather(piece, "sec", axis=0, tiled=True)
    return pair_gather(block, height)


def halve_pairs(partial_sum, height):
    leaf_place = lax.axis_index("leaf")
    for bit_index in reversed(range(height)):
        half_rows = partial_sum.shape[0] // 2
        lower_rows = partial_sum[:half_rows]
        upper_rows = partial_sum[half_rows:]
        upper_half = leaf_place >> bit_index & 1 == 1
        kept = jnp.where(upper_half, upper_rows, lower_rows)
        outgoing = jnp.where(upper_half, lower_rows, upper_rows)
        partial_sum = kept + from_partner(outgoing, "leaf", bit_index)
    return partial_sum


def group_reduce(partial_sum, height):
    reduced = halve_pairs(partial_sum, height)
    return lax.psum_scatter(reduced, "sec", scatter_dimension=0, tiled=True)


def leafwise_on_device(
    leaf_inv,
    subtree_blocks,
    subtree_shift_rhs,
    leaf_noise,
    leaf_dev,
    sep_inv,
    sep_panel,
    sep_rhs,
    sep_noise,
    sep_dev,
):
    subtree_row_count = leaf_inv.shape[0]
    row_count = sep_inv.shape[0]
    levels = sep_rhs.shape[0]
    sections = lax.axis_size("sec")
    active_rows = subtree_blocks[0, 0] * BLOCK
    row_positions = jnp.arange(subtree_row_count, dtype=jnp.int32)
    row_activity = (row_positions >= subtree_row_count - active_rows)[:, None]
    subtree_shifted = jnp.where(
        row_activity, subtree_shift_rhs, jnp.zeros((), subtree_shift_rhs.dtype)
    )
    forward_subtree = jnp.dot(leaf_inv, subtree_shifted, preferred_element_type=jnp.float32)
    subtree_forward_solution = jnp.where(row_activity, forward_subtree, jnp.float32(0.0)).astype(
        jnp.bfloat16
    )
    top = subtree_forward_solution[subtree_row_count - row_count :]
    solved = []
    for height in range(1, levels + 1):
        span = 2**height * sections * row_count
        offset = (2**height - 2) * sections * row_count
        children = group_gather(top, height)
        panel = sep_panel[:, offset : offset + span]
        inverse_block = sep_inv[:, offset : offset + span]
        reduced = (
            sep_rhs[height - 1].astype(jnp.float32)
            - jnp.dot(panel, children, preferred_element_type=jnp.float32)
        ).astype(jnp.bfloat16)
        whole_reduced = group_gather(reduced, height)
        result = jnp.dot(inverse_block, whole_reduced, preferred_element_type=jnp.float32).astype(
            jnp.bfloat16
        )
        solved.append(result)
        top = result
    samples = [None] * levels
    correction = None
    for height in range(levels, 0, -1):
        span = 2**height * sections * row_count
        offset = (2**height - 2) * sections * row_count
        panel = sep_panel[:, offset : offset + span]
        inverse_block = sep_inv[:, offset : offset + span]
        summed = solved[height - 1].astype(jnp.float32) + sep_noise[height - 1].astype(jnp.float32)
        if correction is not None:
            summed = summed - correction
        vector = summed.astype(jnp.bfloat16)
        backed = group_reduce(transposed_dot(inverse_block, vector), height).astype(
            jnp.bfloat16
        )
        samples[height - 1] = (
            sep_dev[height - 1][:, None].astype(jnp.float32) * backed.astype(jnp.float32)
        ).astype(jnp.bfloat16)
        correction = group_reduce(transposed_dot(panel, backed), height)
    leading = jnp.zeros((subtree_row_count - row_count, correction.shape[1]), jnp.float32)
    placed = jnp.concatenate([leading, correction], axis=0)
    subtree_summed = (
        subtree_forward_solution.astype(jnp.float32) + leaf_noise.astype(jnp.float32) - placed
    )
    subtree_weight = jnp.where(row_activity, subtree_summed, jnp.float32(0.0)).astype(jnp.bfloat16)
    subtree_solution = transposed_dot(leaf_inv, subtree_weight)
    sample_scales = leaf_dev[:, None].astype(jnp.float32)
    subtree_scaled_samples = jnp.where(
        row_activity, sample_scales * subtree_solution, jnp.float32(0.0)
    ).astype(jnp.bfloat16)
    return (subtree_scaled_samples, jnp.stack(samples))


def on_device(
    leaf_inv,
    subtree_blocks,
    subtree_shift_rhs,
    leaf_noise,
    leaf_dev,
    sep_inv,
    sep_panel,
    sep_rhs,
    sep_noise,
    sep_dev,
):
    subtree_rows = leaf_inv.shape[0]
    row_count = sep_inv.shape[0]
    levels, _, samples = sep_rhs.shape
    unit = 2 * row_count
    vmem = pl.BlockSpec(memory_space=pltpu.VMEM)
    smem = pl.BlockSpec(memory_space=pltpu.SMEM)

    def params(mib):
        return pltpu.CompilerParams(vmem_limit_bytes=mib * 2**20)

    top_columns = 2 * 2**levels * unit + 2 * samples
    low_columns = samples + sum(2 * 2**h * unit + 2 * samples for h in range(1, levels))
    hbm = pl.BlockSpec(memory_space=pltpu.HBM)

    def in_hbm(array):
        return pltpu.with_memory_space_constraint(array, pltpu.HBM)

    low, top = pl.pallas_call(
        functools.partial(pack_kernel, levels),
        out_shape=(
            jax.ShapeDtypeStruct((row_count, low_columns), jnp.bfloat16),
            jax.ShapeDtypeStruct((row_count, top_columns), jnp.bfloat16),
        ),
        in_specs=[smem] + [hbm] * 6,
        out_specs=(vmem, vmem),
        scratch_shapes=[
            pltpu.VMEM((row_count, subtree_rows), jnp.bfloat16),
            pltpu.VMEM(subtree_shift_rhs.shape, jnp.bfloat16),
            pltpu.VMEM(sep_panel.shape, jnp.bfloat16),
            pltpu.VMEM(sep_inv.shape, jnp.bfloat16),
            pltpu.VMEM(sep_rhs.shape, jnp.bfloat16),
            pltpu.VMEM(sep_noise.shape, jnp.bfloat16),
            pltpu.SemaphoreType.DMA((6,)),
        ],
        compiler_params=params(4),
        name="pack",
    )(subtree_blocks, *(in_hbm(x) for x in (leaf_inv, subtree_shift_rhs, sep_panel, sep_inv, sep_rhs, sep_noise)))

    def swap(block):
        return lax.ppermute(block, "sec", [(0, 1), (1, 0)])

    def join(arrays, *after, flops=0):
        rows = sum(array.shape[0] for array in arrays)
        return pl.pallas_call(
            lambda *refs: join_kernel(*refs[len(after) :]),
            out_shape=jax.ShapeDtypeStruct((rows, arrays[0].shape[1]), arrays[0].dtype),
            in_specs=[pl.BlockSpec(memory_space=pl.ANY)] * len(after) + [vmem] * len(arrays),
            out_specs=vmem,
            compiler_params=params(4),
            cost_estimate=pl.CostEstimate(flops=flops, bytes_accessed=0, transcendentals=0) if flops else None,
            name="join",
        )(*after, *arrays)

    quad = 2 ** (levels - 1)
    near = join([low] + [to_chips(low, (distance, distance)) for distance in range(1, quad)])
    passed = swap(near)
    quarter = []
    for turned, array in enumerate((near, passed)):
        for distance in range(quad):
            quarter.append((array, distance * row_count, (distance, distance), turned))

    top_other = swap(top)
    top_pair = join([top, top_other], flops=10**10)

    def listed(pieces):
        arrays, places = [], []
        for array, start, distances, turned in pieces:
            if not any(array is known for known in arrays):
                arrays.append(array)
            which = [array is known for known in arrays].index(True)
            places.append((which, start, distances, turned))
        return arrays, places

    base, edge, inner, scale, sep_scale = pl.pallas_call(
        functools.partial(leaf_kernel, row_count),
        out_shape=(
            jax.ShapeDtypeStruct((subtree_rows, samples), jnp.float32),
            jax.ShapeDtypeStruct((row_count, samples), jnp.float32),
            jax.ShapeDtypeStruct((subtree_rows, row_count), jnp.bfloat16),
            jax.ShapeDtypeStruct((subtree_rows, samples), jnp.float32),
            jax.ShapeDtypeStruct((levels, row_count, samples), jnp.float32),
        ),
        in_specs=[smem] + [vmem] * 5,
        out_specs=(vmem,) * 5,
        compiler_params=params(12),
        cost_estimate=pl.CostEstimate(flops=10**10, bytes_accessed=1, transcendentals=0),
        name="leaf",
    )(subtree_blocks, leaf_inv, subtree_shift_rhs, leaf_noise, leaf_dev[None, :], sep_dev)

    arrays, places = listed(quarter)
    low_whole, *solved = pl.pallas_call(
        functools.partial(low_kernel, levels, unit, places),
        out_shape=[jax.ShapeDtypeStruct((quad * unit, low_columns), jnp.bfloat16)]
        + [jax.ShapeDtypeStruct((quad * unit, samples), jnp.bfloat16)] * (levels - 1),
        in_specs=[vmem] * len(arrays) + [pl.BlockSpec(memory_space=pl.ANY)],
        out_specs=[vmem] * levels,
        compiler_params=params(8),
        name="low",
    )(*arrays, edge)
    partner = to_chips(solved[-1], (quad, quad))

    trips = [(join([top], top_pair), (1, 1)), (top_pair, (3, 2)), (top_pair, (4, 5)), (top_pair, (6, 7))]
    far = [(top, 0, (0, 0), 0), (top_other, 0, (0, 0), 1)]
    arrived = [to_chips(block, distances) for block, distances in trips]
    for chosen in ((2, 3, 0), (1,)):
        here = join([arrived[index] for index in chosen], solved[-1])
        there = swap(here)
        row = 0
        for block, (first, second) in (trips[index] for index in chosen):
            for turned in range(block.shape[0] // row_count):
                far.append((here, row, (first, second), turned))
                far.append((there, row, (second, first), 1 - turned))
                row += row_count

    edge = join([edge], partner, flops=10**10)
    arrays, places = listed(far)
    span = 2**levels * unit
    return pl.pallas_call(
        functools.partial(top_kernel, levels, unit, places),
        out_shape=(
            jax.ShapeDtypeStruct((subtree_rows, samples), jnp.bfloat16),
            jax.ShapeDtypeStruct((levels, row_count, samples), jnp.bfloat16),
        ),
        in_specs=[vmem] * (7 + levels - 1 + len(arrays)),
        out_specs=(vmem, vmem),
        scratch_shapes=[
            pltpu.VMEM((span, top_columns), jnp.bfloat16),
            pltpu.VMEM((span, samples), jnp.bfloat16),
            pltpu.VMEM((span, samples), jnp.float32),
            pltpu.VMEM((unit * 2, samples), jnp.float32),
        ],
        compiler_params=params(16),
        name="top",
    )(low_whole, sep_scale, partner, base, edge, inner, scale, *solved, *arrays)


def solution(mesh):
    rows = P(AXES, None)
    in_specs = (
        rows,
        P("leaf", "sec"),
        rows,
        rows,
        P(AXES),
        rows,
        rows,
        P(None, AXES, None),
        P(None, AXES, None),
        P(None, AXES),
    )
    out_specs = (rows, P(None, AXES, None))

    def program(*arrays):
        levels = arrays[7].shape[0]
        paired = levels == 3 and mesh.shape["sec"] == 2 and mesh.shape["leaf"] % 2**levels == 0
        return on_device(*arrays) if paired else leafwise_on_device(*arrays)

    return jax.shard_map(program, mesh=mesh, in_specs=in_specs, out_specs=out_specs, check_vma=False)
```

```python
import functools

import jax
import jax.numpy as jnp
from jax import lax
from jax.experimental import pallas as pl
from jax.experimental.pallas import tpu as pltpu
from jax.sharding import PartitionSpec as P

BLOCK = 128
AXES = ("leaf", "sec")


def to_chips(block, distances):
    leaves, sections = lax.axis_size("leaf"), lax.axis_size("sec")
    route = []
    for leaf in range(leaves):
        for section, distance in enumerate(distances):
            route.append((leaf * sections + section, (leaf ^ distance) * sections + section))
    return lax.ppermute(block, AXES, route)


def column_of(row):
    count = row.shape[1]
    across = lax.broadcasted_iota(jnp.int32, (count, count), 1)
    down = lax.broadcasted_iota(jnp.int32, (count, count), 0)
    return jnp.sum(jnp.where(across == down, row, jnp.zeros_like(row)), axis=1, keepdims=True)


def live_rows(blocks_ref, shape, dimension):
    return lax.broadcasted_iota(jnp.int32, shape, dimension) >= shape[dimension] - blocks_ref[0, 0] * BLOCK


def pack_kernel(levels, blocks_ref, *refs):
    sources, (low_ref, top_ref), moved, arrived = refs[:6], refs[6:8], refs[8:14], refs[14]
    rows = sources[0].shape[0]
    row_count = moved[0].shape[0]
    parts = (sources[0].at[pl.ds(rows - row_count, row_count)],) + sources[1:]
    copies = [pltpu.make_async_copy(part, ref, arrived.at[n]) for n, (part, ref) in enumerate(zip(parts, moved))]
    for copy in copies:
        copy.start()
    edge_ref, shift_ref, panel_ref, inv_ref, rhs_ref, noise_ref = moved
    samples = shift_ref.shape[1]
    for copy in copies[2:]:
        copy.wait()
    unit = panel_ref.shape[1] // (2 ** (levels + 1) - 2)
    at, offset = samples, 0
    for height in range(1, levels + 1):
        span = 2**height * unit
        out = low_ref if height < levels else top_ref
        at = at if height < levels else 0
        out[:, at : at + span] = panel_ref[:, offset : offset + span]
        out[:, at + span : at + 2 * span] = inv_ref[:, offset : offset + span]
        out[:, at + 2 * span : at + 2 * span + samples] = rhs_ref[height - 1]
        out[:, at + 2 * span + samples : at + 2 * span + 2 * samples] = noise_ref[height - 1]
        at += 2 * span + 2 * samples
        offset += span
    for copy in copies[:2]:
        copy.wait()
    inverse = edge_ref[...]
    inverse = jnp.where(live_rows(blocks_ref, inverse.shape, 1), inverse, jnp.zeros_like(inverse))
    boundary = jnp.dot(inverse, shift_ref[...], preferred_element_type=jnp.float32)
    low_ref[:, :samples] = boundary.astype(jnp.bfloat16)


def join_kernel(*refs):
    joined_ref, row = refs[-1], 0
    for ref in refs[:-1]:
        joined_ref[row : row + ref.shape[0], :] = ref[...]
        row += ref.shape[0]


def place(pieces, refs, whole_ref, row_count, leaves):
    leaf, section = lax.axis_index("leaf"), lax.axis_index("sec")
    for which, start, distances, turned in pieces:
        if isinstance(turned, int):
            owner = section ^ turned
            distance = jnp.where(section == 0, distances[0], distances[1])
        else:
            owner, distance = turned[0], distances[0]
        at = (((leaf ^ distance) & (leaves - 1)) * 2 + owner) * row_count
        ref = refs[which]
        whole_ref[pl.ds(pl.multiple_of(at, row_count), row_count), :] = ref[start : start + row_count, :]


def solve_forward(whole, rows, at, span, samples, children):
    panel = whole[rows, at : at + span]
    inverse = whole[rows, at + span : at + 2 * span]
    rhs = whole[rows, at + 2 * span : at + 2 * span + samples]
    reduced = rhs.astype(jnp.float32) - jnp.dot(panel, children, preferred_element_type=jnp.float32)
    reduced = reduced.astype(jnp.bfloat16)
    return jnp.dot(inverse, reduced, preferred_element_type=jnp.float32).astype(jnp.bfloat16)


def low_kernel(levels, unit, pieces, *refs):
    piece_refs, (whole_ref, *solved_refs) = refs[: -levels - 1], refs[-levels:]
    row_count = unit // 2
    place(pieces, piece_refs, whole_ref, row_count, 2 ** (levels - 1))
    samples = solved_refs[-1].shape[0]
    total = whole_ref.shape[0]
    below_ref, at = whole_ref, samples
    for height in range(1, levels):
        span = 2**height * unit
        for group in range(total // span):
            rows = slice(group * span, (group + 1) * span)
            children = below_ref[rows, 0:samples]
            solved = solve_forward(whole_ref, rows, at, span, samples, children)
            if height < levels - 1:
                solved_refs[height - 1][rows, :] = solved
            else:
                solved_refs[height - 1][:, rows] = solved.astype(jnp.float32).T.astype(jnp.bfloat16)
        below_ref = solved_refs[height - 1]
        at += 2 * span + 2 * samples


def leaf_kernel(
    row_count,
    blocks_ref,
    leaf_ref,
    shift_ref,
    noise_ref,
    dev_ref,
    sep_dev_ref,
    base_ref,
    edge_ref,
    inner_ref,
    scale_ref,
    sep_scale_ref,
):
    rows, samples = shift_ref.shape
    live = live_rows(blocks_ref, (rows, samples), 0)
    shift = shift_ref[...]
    shift = jnp.where(live, shift, jnp.zeros_like(shift))
    zero = jnp.float32(0.0)
    forward = jnp.dot(leaf_ref[...], shift, preferred_element_type=jnp.float32)
    forward = jnp.where(live, forward, zero).astype(jnp.bfloat16)
    summed = forward.astype(jnp.float32) + noise_ref[...].astype(jnp.float32)
    inner = rows - row_count
    edge_ref[...] = summed[inner:, :]
    within = lax.broadcasted_iota(jnp.int32, (rows, samples), 0) < inner
    weight = jnp.where(live & within, summed, zero)
    product = jnp.dot(weight.T.astype(jnp.bfloat16), leaf_ref[...], preferred_element_type=jnp.float32)
    base_ref[...] = product.T
    inner_ref[...] = leaf_ref[inner:, :].astype(jnp.float32).T.astype(jnp.bfloat16)
    deviations = dev_ref[...].astype(jnp.float32)
    sep_deviations = sep_dev_ref[...].astype(jnp.float32)
    for block in range(rows // BLOCK):
        part = slice(block * BLOCK, (block + 1) * BLOCK)
        column = column_of(deviations[:, part])
        scale_ref[part, :] = jnp.where(live[part, :], jnp.broadcast_to(column, (BLOCK, samples)), zero)
    for height in range(sep_scale_ref.shape[0]):
        column = column_of(sep_deviations[height : height + 1, :])
        sep_scale_ref[height] = jnp.broadcast_to(column, (row_count, samples))


def top_kernel(levels, unit, pieces, *refs):
    low_ref, sep_scale_ref, partner_ref, base_ref, edge_ref, inner_ref, scale_ref = refs[:7]
    solved_refs = refs[7 : 7 + levels - 1]
    out_ref, sample_ref, whole_ref, x_ref, sum_ref = refs[-5:]
    piece_refs = refs[7 + levels - 1 : -5]
    samples = partner_ref.shape[0]
    row_count = unit // 2
    leaf, section = lax.axis_index("leaf"), lax.axis_index("sec")
    place(pieces, piece_refs, whole_ref, row_count, 2**levels)
    upper = leaf >> (levels - 1) & 1
    mine, theirs = solved_refs[-1][...], partner_ref[...]
    children = jnp.concatenate([jnp.where(upper == 1, theirs, mine), jnp.where(upper == 1, mine, theirs)], axis=1)
    top_span = 2**levels * unit
    across = (((1,), (1,)), ((), ()))
    rhs = whole_ref[:, 2 * top_span : 2 * top_span + samples].astype(jnp.float32).T
    reduced = rhs - lax.dot_general(
        children, whole_ref[:, 0:top_span], across, preferred_element_type=jnp.float32
    )
    own = lax.dot_general(
        reduced.astype(jnp.bfloat16),
        whole_ref[:, top_span : 2 * top_span],
        across,
        preferred_element_type=jnp.float32,
    ).astype(jnp.bfloat16)
    correction = None
    low_at = low_ref.shape[1]
    for height in range(levels, 0, -1):
        span = 2**height * unit
        if height == levels:
            source, at, rows = whole_ref, 0, slice(0, span)
        else:
            low_at -= 2 * span + 2 * samples
            first = ((leaf & (2 ** (levels - 1) - 1)) >> height) * span
            source, at, rows = low_ref, low_at, pl.ds(pl.multiple_of(first, span), span)
            own = solved_refs[height - 1][...] if height == levels - 1 else solved_refs[height - 1][rows, :]
        noise = source[rows, at + 2 * span + samples : at + 2 * span + 2 * samples]
        if height >= levels - 1:
            summed = own.astype(jnp.float32) + noise.astype(jnp.float32).T
        else:
            summed = (own.astype(jnp.float32) + noise.astype(jnp.float32)).T
        if correction is not None:
            summed = summed - correction
        x = jnp.dot(
            summed.astype(jnp.bfloat16), source[rows, at + span : at + 2 * span], preferred_element_type=jnp.float32
        ).astype(jnp.bfloat16)
        pushed = jnp.dot(x, source[rows, at : at + span], preferred_element_type=jnp.float32)
        x_ref[0:span, :] = x.astype(jnp.float32).T
        mine = pl.ds(pl.multiple_of(((leaf & (2**height - 1)) * 2 + section) * row_count, row_count), row_count)
        sample_ref[height - 1] = (sep_scale_ref[height - 1] * x_ref[mine, :]).astype(jnp.bfloat16)
        if height > 1:
            upper = leaf >> (height - 1) & 1
            correction = jnp.where(upper == 1, pushed[:, span // 2 :], pushed[:, : span // 2])
        else:
            sum_ref[...] = pushed.T
            correction = sum_ref[mine, :]
    weight = (edge_ref[...] - correction).astype(jnp.bfloat16)
    back = base_ref[...] + jnp.dot(inner_ref[...], weight, preferred_element_type=jnp.float32)
    out_ref[...] = (scale_ref[...] * back).astype(jnp.bfloat16)


def transposed_dot(matrix, vector):
    return lax.dot_general(matrix, vector, (((0,), (0,)), ((), ())), preferred_element_type=jnp.float32)


def from_partner(block, axis, apart):
    count = lax.axis_size(axis)
    route = []
    for low in range(count):
        high = low | 1 << apart
        if high != low and high < count:
            route += [(low, high), (high, low)]
    return lax.ppermute(block, axis, route)


def pair_gather(block, height):
    leaf_place = lax.axis_index("leaf")
    for bit_index in range(height):
        partner = from_partner(block, "leaf", bit_index)
        upper_half = leaf_place >> bit_index & 1 == 1
        block = jnp.where(
            upper_half, jnp.concatenate([partner, block], 0), jnp.concatenate([block, partner], 0)
        )
    return block


def group_gather(piece, height):
    block = lax.all_gather(piece, "sec", axis=0, tiled=True)
    return pair_gather(block, height)


def halve_pairs(partial_sum, height):
    leaf_place = lax.axis_index("leaf")
    for bit_index in reversed(range(height)):
        half_rows = partial_sum.shape[0] // 2
        lower_rows = partial_sum[:half_rows]
        upper_rows = partial_sum[half_rows:]
        upper_half = leaf_place >> bit_index & 1 == 1
        kept = jnp.where(upper_half, upper_rows, lower_rows)
        outgoing = jnp.where(upper_half, lower_rows, upper_rows)
        partial_sum = kept + from_partner(outgoing, "leaf", bit_index)
    return partial_sum


def group_reduce(partial_sum, height):
    reduced = halve_pairs(partial_sum, height)
    return lax.psum_scatter(reduced, "sec", scatter_dimension=0, tiled=True)


def leafwise_on_device(
    leaf_inv,
    subtree_blocks,
    subtree_shift_rhs,
    leaf_noise,
    leaf_dev,
    sep_inv,
    sep_panel,
    sep_rhs,
    sep_noise,
    sep_dev,
):
    subtree_row_count = leaf_inv.shape[0]
    row_count = sep_inv.shape[0]
    levels = sep_rhs.shape[0]
    sections = lax.axis_size("sec")
    active_rows = subtree_blocks[0, 0] * BLOCK
    row_positions = jnp.arange(subtree_row_count, dtype=jnp.int32)
    row_activity = (row_positions >= subtree_row_count - active_rows)[:, None]
    subtree_shifted = jnp.where(
        row_activity, subtree_shift_rhs, jnp.zeros((), subtree_shift_rhs.dtype)
    )
    forward_subtree = jnp.dot(leaf_inv, subtree_shifted, preferred_element_type=jnp.float32)
    subtree_forward_solution = jnp.where(row_activity, forward_subtree, jnp.float32(0.0)).astype(
        jnp.bfloat16
    )
    top = subtree_forward_solution[subtree_row_count - row_count :]
    solved = []
    for height in range(1, levels + 1):
        span = 2**height * sections * row_count
        offset = (2**height - 2) * sections * row_count
        children = group_gather(top, height)
        panel = sep_panel[:, offset : offset + span]
        inverse_block = sep_inv[:, offset : offset + span]
        reduced = (
            sep_rhs[height - 1].astype(jnp.float32)
            - jnp.dot(panel, children, preferred_element_type=jnp.float32)
        ).astype(jnp.bfloat16)
        whole_reduced = group_gather(reduced, height)
        result = jnp.dot(inverse_block, whole_reduced, preferred_element_type=jnp.float32).astype(
            jnp.bfloat16
        )
        solved.append(result)
        top = result
    samples = [None] * levels
    correction = None
    for height in range(levels, 0, -1):
        span = 2**height * sections * row_count
        offset = (2**height - 2) * sections * row_count
        panel = sep_panel[:, offset : offset + span]
        inverse_block = sep_inv[:, offset : offset + span]
        summed = solved[height - 1].astype(jnp.float32) + sep_noise[height - 1].astype(jnp.float32)
        if correction is not None:
            summed = summed - correction
        vector = summed.astype(jnp.bfloat16)
        backed = group_reduce(transposed_dot(inverse_block, vector), height).astype(
            jnp.bfloat16
        )
        samples[height - 1] = (
            sep_dev[height - 1][:, None].astype(jnp.float32) * backed.astype(jnp.float32)
        ).astype(jnp.bfloat16)
        correction = group_reduce(transposed_dot(panel, backed), height)
    leading = jnp.zeros((subtree_row_count - row_count, correction.shape[1]), jnp.float32)
    placed = jnp.concatenate([leading, correction], axis=0)
    subtree_summed = (
        subtree_forward_solution.astype(jnp.float32) + leaf_noise.astype(jnp.float32) - placed
    )
    subtree_weight = jnp.where(row_activity, subtree_summed, jnp.float32(0.0)).astype(jnp.bfloat16)
    subtree_solution = transposed_dot(leaf_inv, subtree_weight)
    sample_scales = leaf_dev[:, None].astype(jnp.float32)
    subtree_scaled_samples = jnp.where(
        row_activity, sample_scales * subtree_solution, jnp.float32(0.0)
    ).astype(jnp.bfloat16)
    return (subtree_scaled_samples, jnp.stack(samples))


def on_device(
    leaf_inv,
    subtree_blocks,
    subtree_shift_rhs,
    leaf_noise,
    leaf_dev,
    sep_inv,
    sep_panel,
    sep_rhs,
    sep_noise,
    sep_dev,
):
    subtree_rows = leaf_inv.shape[0]
    row_count = sep_inv.shape[0]
    levels, _, samples = sep_rhs.shape
    unit = 2 * row_count
    vmem = pl.BlockSpec(memory_space=pltpu.VMEM)
    smem = pl.BlockSpec(memory_space=pltpu.SMEM)

    def params(mib):
        return pltpu.CompilerParams(vmem_limit_bytes=mib * 2**20)

    top_columns = 2 * 2**levels * unit + 2 * samples
    low_columns = samples + sum(2 * 2**h * unit + 2 * samples for h in range(1, levels))
    hbm = pl.BlockSpec(memory_space=pltpu.HBM)

    def in_hbm(array):
        return pltpu.with_memory_space_constraint(array, pltpu.HBM)

    low, top = pl.pallas_call(
        functools.partial(pack_kernel, levels),
        out_shape=(
            jax.ShapeDtypeStruct((row_count, low_columns), jnp.bfloat16),
            jax.ShapeDtypeStruct((row_count, top_columns), jnp.bfloat16),
        ),
        in_specs=[smem] + [hbm] * 6,
        out_specs=(vmem, vmem),
        scratch_shapes=[
            pltpu.VMEM((row_count, subtree_rows), jnp.bfloat16),
            pltpu.VMEM(subtree_shift_rhs.shape, jnp.bfloat16),
            pltpu.VMEM(sep_panel.shape, jnp.bfloat16),
            pltpu.VMEM(sep_inv.shape, jnp.bfloat16),
            pltpu.VMEM(sep_rhs.shape, jnp.bfloat16),
            pltpu.VMEM(sep_noise.shape, jnp.bfloat16),
            pltpu.SemaphoreType.DMA((6,)),
        ],
        compiler_params=params(4),
        name="pack",
    )(subtree_blocks, *(in_hbm(x) for x in (leaf_inv, subtree_shift_rhs, sep_panel, sep_inv, sep_rhs, sep_noise)))

    def swap(block):
        return lax.ppermute(block, "sec", [(0, 1), (1, 0)])

    def join(arrays, *after, flops=0):
        rows = sum(array.shape[0] for array in arrays)
        return pl.pallas_call(
            lambda *refs: join_kernel(*refs[len(after) :]),
            out_shape=jax.ShapeDtypeStruct((rows, arrays[0].shape[1]), arrays[0].dtype),
            in_specs=[pl.BlockSpec(memory_space=pl.ANY)] * len(after) + [vmem] * len(arrays),
            out_specs=vmem,
            compiler_params=params(4),
            cost_estimate=pl.CostEstimate(flops=flops, bytes_accessed=0, transcendentals=0) if flops else None,
            name="join",
        )(*after, *arrays)

    quad = 2 ** (levels - 1)
    near = join([low] + [to_chips(low, (distance, distance)) for distance in range(1, quad)])
    passed = swap(near)
    quarter = []
    for turned, array in enumerate((near, passed)):
        for distance in range(quad):
            quarter.append((array, distance * row_count, (distance, distance), turned))

    top_other = swap(top)
    top_pair = join([top, top_other], flops=10**10)

    def listed(pieces):
        arrays, places = [], []
        for array, start, distances, turned in pieces:
            if not any(array is known for known in arrays):
                arrays.append(array)
            which = [array is known for known in arrays].index(True)
            places.append((which, start, distances, turned))
        return arrays, places

    base, edge, inner, scale, sep_scale = pl.pallas_call(
        functools.partial(leaf_kernel, row_count),
        out_shape=(
            jax.ShapeDtypeStruct((subtree_rows, samples), jnp.float32),
            jax.ShapeDtypeStruct((row_count, samples), jnp.float32),
            jax.ShapeDtypeStruct((subtree_rows, row_count), jnp.bfloat16),
            jax.ShapeDtypeStruct((subtree_rows, samples), jnp.float32),
            jax.ShapeDtypeStruct((levels, row_count, samples), jnp.float32),
        ),
        in_specs=[smem] + [vmem] * 5,
        out_specs=(vmem,) * 5,
        compiler_params=params(12),
        cost_estimate=pl.CostEstimate(flops=10**10, bytes_accessed=1, transcendentals=0),
        name="leaf",
    )(subtree_blocks, leaf_inv, subtree_shift_rhs, leaf_noise, leaf_dev[None, :], sep_dev)

    arrays, places = listed(quarter)
    low_whole, *solved = pl.pallas_call(
        functools.partial(low_kernel, levels, unit, places),
        out_shape=[jax.ShapeDtypeStruct((quad * unit, low_columns), jnp.bfloat16)]
        + [jax.ShapeDtypeStruct((quad * unit, samples), jnp.bfloat16)] * (levels - 2)
        + [jax.ShapeDtypeStruct((samples, quad * unit), jnp.bfloat16)],
        in_specs=[vmem] * len(arrays) + [pl.BlockSpec(memory_space=pl.ANY)],
        out_specs=[vmem] * levels,
        compiler_params=params(8),
        name="low",
    )(*arrays, edge)
    partner = to_chips(solved[-1], (quad, quad))

    trips = [(join([top], top_pair), (1, 1)), (top_pair, (3, 2)), (top_pair, (4, 5)), (top_pair, (6, 7))]
    far = [(top, 0, (0, 0), 0), (top_other, 0, (0, 0), 1)]
    arrived = [to_chips(block, distances) for block, distances in trips]
    for chosen in ((2, 3, 0), (1,)):
        here = join([arrived[index] for index in chosen], solved[-1])
        there = swap(here)
        row = 0
        for block, (first, second) in (trips[index] for index in chosen):
            for turned in range(block.shape[0] // row_count):
                far.append((here, row, (first, second), turned))
                far.append((there, row, (second, first), 1 - turned))
                row += row_count

    edge = join([edge], partner, flops=10**10)
    arrays, places = listed(far)
    span = 2**levels * unit
    return pl.pallas_call(
        functools.partial(top_kernel, levels, unit, places),
        out_shape=(
            jax.ShapeDtypeStruct((subtree_rows, samples), jnp.bfloat16),
            jax.ShapeDtypeStruct((levels, row_count, samples), jnp.bfloat16),
        ),
        in_specs=[vmem] * (7 + levels - 1 + len(arrays)),
        out_specs=(vmem, vmem),
        scratch_shapes=[
            pltpu.VMEM((span, top_columns), jnp.bfloat16),
            pltpu.VMEM((span, samples), jnp.float32),
            pltpu.VMEM((unit * 2, samples), jnp.float32),
        ],
        compiler_params=params(16),
        name="top",
    )(low_whole, sep_scale, partner, base, edge, inner, scale, *solved, *arrays)


def solution(mesh):
    rows = P(AXES, None)
    in_specs = (
        rows,
        P("leaf", "sec"),
        rows,
        rows,
        P(AXES),
        rows,
        rows,
        P(None, AXES, None),
        P(None, AXES, None),
        P(None, AXES),
    )
    out_specs = (rows, P(None, AXES, None))

    def program(*arrays):
        levels = arrays[7].shape[0]
        paired = levels == 3 and mesh.shape["sec"] == 2 and mesh.shape["leaf"] % 2**levels == 0
        return on_device(*arrays) if paired else leafwise_on_device(*arrays)

    return jax.shard_map(program, mesh=mesh, in_specs=in_specs, out_specs=out_specs, check_vma=False)
```
